32 devices in a mesh: grid: 4 (over z), space: 4 (over y, x), spec: 2 (over core).
Axes of the slice: x: 2, y: 2, z: 4, core: 2. Of those that a mesh axis runs over, the one named last changes fastest.
Arguments:
- spectrum: float32 [4, 32, 36, 8, 128], P('grid', None, None, ('space', 'spec')), may hold values from 0.05 to 1
- land_sea: int32 [4, 8, 128], P('grid'), may hold values 0 or 1
- west_index: int32 [4, 8], P('grid'), may hold values from 0 to 7, each once within a row
- east_index: int32 [4, 8], P('grid'), may hold values from 0 to 7, each once within a row
- current_u: float32 [4, 64, 8, 128], P('grid', None, ('space', 'spec')), may hold values from -0.3 to 0.3
- current_v: float32 [4, 64, 8, 128], P('grid', None, ('space', 'spec')), may hold values from -0.3 to 0.3
- transfer: bfloat16 [1152, 1152], replicated, may hold values from -0.1875 to 0.1875
- wind_rate: float32 [36], replicated, may hold values from 0.1 to 1
- dissipation: float32 [36], replicated, may hold values from 0.5 to 4
Outputs:
- waves: float32 [4, 32, 36, 8, 128], P('grid', 'space', 'spec')
- stokes: float32 [4, 128, 8, 128], P('grid', None, ('space', 'spec'))
The draws below stay inside these ranges and needn't reach their ends.
Inputs may be any that keep to these rules, and one draw needn't show every extreme that they name: `land_sea`: 1 marks a sea cell, 0 a land cell. `west_index`: row g lists, for each row of grid g, the row of grid g - 1 whose easternmost cell borders it; each row of the array is a permutation of the 8 rows. `east_index`: row g lists, for each row of grid g, the row of grid g + 1 whose westernmost cell borders it; each row of the array is a permutation of the 8 rows.
All inputs are finite; a program needn't handle non-finite values. No bound on the sum of `land_sea` on one device may be relied on, other than what follows from the above.
Results may differ from the reference program's by a relative error of at most 0.00082.
Values sent between devices are 32-bit elements; how exact they have to be, the bound alone decides.
A program may use at most 64 MiB of HBM per device.

```python
import math
import jax
import jax.numpy as jnp
from jax import lax

ND = 32
NF = 36
LEV = 64
NCOL = 128
SUBSTEPS = 1
NGRID = 4
NROW = 8
COMPS = 1152


def place_ends(drawn, rng, least, largest):
    dims = drawn.shape
    spot = [jax.random.randint(jax.random.fold_in(rng, axis), (), 0, dims[axis]) for axis in range(len(dims))]
    drawn = drawn.at[tuple(spot)].set(least)
    longest = dims.index(max(dims))
    spot[longest] = (spot[longest] + 1) % dims[longest]
    return drawn.at[tuple(spot)].set(largest)


def block_scale(stream_key, extent, shards, least, top_value):
    level = 1.0
    for axis_at, shards_of in shards:
        heights = jax.random.uniform(jax.random.fold_in(jax.random.fold_in(stream_key, 6), axis_at), (shards_of,), jnp.float32, least / len(shards), top_value / len(shards))
        level = level * jnp.repeat(jnp.exp(heights), extent[axis_at] // shards_of).reshape((-1,) + (1,) * (len(extent) - 1 - axis_at))
    return level


def bell_draw(own_key, extent, spread, reach, held_as=jnp.bfloat16):
    result = jax.random.normal(own_key, extent, jnp.float32) * spread
    return jnp.minimum(jnp.maximum(result, -reach), reach).astype(held_as)


def setup_inputs(seed: int = 0) -> dict:
    keys = jax.random.split(jax.random.key(seed), 10)
    return {
        "spectrum": jnp.clip(jnp.exp(math.log(1.0) - 2.9957323 * jax.random.uniform(keys[0], (NGRID, ND, NF, NROW, NCOL), jnp.float32) ** block_scale(keys[0], (NGRID, ND, NF, NROW, NCOL), ((0, 4), (3, 8)), -0.2, 0.2)), 0.05, 1.0),
        "land_sea": place_ends((jax.random.randint(keys[1], (NGRID, NROW, NCOL), 0, 5) < 4).astype(jnp.int32), jax.random.fold_in(keys[1], 1), 0, 1),
        "west_index": jax.vmap(lambda own: jax.random.permutation(own, NROW))(jax.random.split(keys[2], NGRID)).reshape((NGRID, NROW)).astype(jnp.int32),
        "east_index": jax.vmap(lambda own: jax.random.permutation(own, NROW))(jax.random.split(keys[3], NGRID)).reshape((NGRID, NROW)).astype(jnp.int32),
        "current_u": jnp.clip(jax.random.uniform(keys[4], (NGRID, LEV, NROW, NCOL), jnp.float32, -0.3, 0.3) * block_scale(keys[4], (NGRID, LEV, NROW, NCOL), ((0, 4), (2, 8)), -0.4, 0.0), -0.3, 0.3),
        "current_v": jnp.clip(jax.random.uniform(keys[5], (NGRID, LEV, NROW, NCOL), jnp.float32, -0.3, 0.3) * block_scale(keys[5], (NGRID, LEV, NROW, NCOL), ((0, 4), (2, 8)), -0.4, 0.0), -0.3, 0.3),
        "transfer": bell_draw(keys[6], (COMPS, COMPS), COMPS ** -0.5, 0.1875),
        "wind_rate": jnp.clip(jnp.exp(jax.random.uniform(keys[7], (NF,), jnp.float32, math.log(0.1), math.log(1.0))), 0.1, 1.0),
        "dissipation": jnp.clip(jnp.exp(jax.random.uniform(keys[8], (NF,), jnp.float32, math.log(0.5), math.log(4.0))), 0.5, 4.0),
    }


sigma_base = 0.2199
gravity = 9.81
growth = 1.1
courant_scale = 3.0
time_step = 0.5
stokes_gain = 2.0
highest = lax.Precision.HIGHEST

def tables(freq_count, directions, levels):
    freq_steps = jnp.arange(freq_count).astype(jnp.float32)
    radian_freq = sigma_base * growth ** freq_steps
    wavenum = radian_freq * radian_freq / gravity
    speeds = courant_scale * growth ** (-freq_steps)
    angles = 2.0 * jnp.pi * jnp.arange(directions).astype(jnp.float32) / directions
    depths = -(jnp.arange(levels).astype(jnp.float32) + 0.5)
    decays = jnp.exp(2.0 * wavenum[:, None] * depths[None, :])
    current_weight = decays / lax.optimization_barrier(jnp.sum(decays, axis=1, keepdims=True))
    drifts = (radian_freq * wavenum)[:, None] * decays
    drifts = drifts / lax.optimization_barrier(jnp.sum(drifts, axis=0, keepdims=True))
    return (speeds, angles, current_weight, drifts)

def sweep_matrix(courant, length):
    forward = jnp.maximum(courant, 0.0)[..., None, None]
    backward = jnp.maximum(-courant, 0.0)[..., None, None]
    places = jnp.arange(length)
    offset = (places[:, None] - places[None, :]).astype(courant.dtype)
    lower_part = jnp.where(offset >= 0, (forward / (1.0 + forward)) ** jnp.maximum(offset, 0.0) / (1.0 + forward), 0.0)
    upper_part = jnp.where(offset <= 0, (backward / (1.0 + backward)) ** jnp.maximum(-offset, 0.0) / (1.0 + backward), 0.0)
    return lower_part + upper_part - jnp.eye(length, dtype=courant.dtype)

def sources(spectra, sea_points, transfer, wind_gain, damping):
    for substep in range(SUBSTEPS):
        rounded = spectra.astype(jnp.bfloat16)
        redist = jnp.dot(transfer, rounded, preferred_element_type=jnp.float32)
        energy = lax.optimization_barrier(jnp.mean(spectra * spectra, axis=0, keepdims=True))
        spectra = sea_points * (spectra * (1.0 + time_step * wind_gain) + time_step * redist) / (1.0 + time_step * damping * energy)
    return spectra

def propagate(wave_field, ghost_west, ghost_east, flow_field, sea_cells, sweep_cols, sweep_rows, courant_x):
    flow_x = flow_field[0][None]
    flow_y = flow_field[1][None]
    west_cells = jnp.concatenate([ghost_west[..., None], wave_field[..., :-1]], axis=-1)
    east_cells = jnp.concatenate([wave_field[..., 1:], ghost_east[..., None]], axis=-1)
    blank_row = jnp.zeros_like(wave_field[..., :1, :])
    north_cells = jnp.concatenate([blank_row, wave_field[..., :-1, :]], axis=-2)
    south_cells = jnp.concatenate([wave_field[..., 1:, :], blank_row], axis=-2)
    moved = wave_field - jnp.maximum(flow_x, 0.0) * (wave_field - west_cells) - jnp.maximum(-flow_x, 0.0) * (wave_field - east_cells) - jnp.maximum(flow_y, 0.0) * (wave_field - north_cells) - jnp.maximum(-flow_y, 0.0) * (wave_field - south_cells)
    inflow_west = jnp.maximum(courant_x, 0.0)[..., None] * ghost_west
    inflow_east = jnp.maximum(-courant_x, 0.0)[..., None] * ghost_east
    moved = moved.at[..., 0].add(inflow_west).at[..., -1].add(inflow_east)
    swept = jnp.einsum('abij,abyj->abyi', sweep_cols, moved, precision=highest)
    swept = jnp.einsum('abij,abjx->abix', sweep_rows, swept, precision=highest)
    return sea_cells * swept

def ghosts(wave_all, west_index, east_index):
    east_cols = wave_all[..., -1]
    west_cols = wave_all[..., 0]
    from_left = jnp.concatenate([jnp.zeros_like(east_cols[:1]), east_cols[:-1]], axis=0)
    from_right = jnp.concatenate([west_cols[1:], jnp.zeros_like(west_cols[:1])], axis=0)
    pick_west = jnp.broadcast_to(west_index[:, None, None, :], from_left.shape)
    pick_east = jnp.broadcast_to(east_index[:, None, None, :], from_right.shape)
    return (jnp.take_along_axis(from_left, pick_west, axis=3), jnp.take_along_axis(from_right, pick_east, axis=3))

def reference(spectrum, land_sea, west_index, east_index, current_u, current_v, transfer, wind_rate, dissipation):
    speeds, angles, current_weight, drifts = tables(NF, ND, LEV)
    courant_x = speeds[None, :] * jnp.cos(angles)[:, None]
    courant_y = speeds[None, :] * jnp.sin(angles)[:, None]
    sweep_cols = sweep_matrix(courant_x, NCOL)
    sweep_rows = sweep_matrix(courant_y, NROW)
    wind_gain = (0.5 * (1.0 + jnp.cos(angles))[:, None] * wind_rate[None, :]).reshape(COMPS, 1)
    damping = jnp.broadcast_to(dissipation[None, :], (ND, NF)).reshape(COMPS, 1)
    drift_x = drifts.T[:, None, :] * (jnp.cos(angles) * stokes_gain / math.sqrt(ND))[None, :, None]
    drift_y = drifts.T[:, None, :] * (jnp.sin(angles) * stokes_gain / math.sqrt(ND))[None, :, None]
    stokes_table = jnp.concatenate([drift_x, drift_y], 0).reshape(2 * LEV, COMPS)
    sea_all = land_sea.astype(jnp.float32)
    flow_all = jnp.stack([jnp.einsum('fl,glyx->gfyx', current_weight, current_u, precision=highest), jnp.einsum('fl,glyx->gfyx', current_weight, current_v, precision=highest)], axis=1)

    def first_sources(grid_pair):
        wave_grid, sea_grid = grid_pair
        updated = sources(wave_grid.reshape(COMPS, NROW * NCOL), sea_grid.reshape(1, NROW * NCOL), transfer, wind_gain, damping)
        return updated.reshape(ND, NF, NROW, NCOL)

    def second_sources(grid_pair):
        wave_grid, sea_grid = grid_pair
        updated = sources(wave_grid.reshape(COMPS, NROW * NCOL), sea_grid.reshape(1, NROW * NCOL), transfer, wind_gain, damping)
        drift_grid = jnp.dot(stokes_table, updated, precision=highest)
        return (updated.reshape(ND, NF, NROW, NCOL), drift_grid.reshape(2 * LEV, NROW, NCOL))

    def propagate_grid(grid_args):
        wave_grid, ghost_west, ghost_east, flow_grid, sea_grid = grid_args
        return propagate(wave_grid, ghost_west, ghost_east, flow_grid, sea_grid, sweep_cols, sweep_rows, courant_x)
    after_sources = lax.map(first_sources, (spectrum, sea_all))
    ghost_west, ghost_east = ghosts(after_sources, west_index, east_index)
    after_first = lax.map(propagate_grid, (after_sources, ghost_west, ghost_east, flow_all, sea_all))
    after_second, stokes = lax.map(second_sources, (after_first, sea_all))
    ghost_west, ghost_east = ghosts(after_second, west_index, east_index)
    waves = lax.map(propagate_grid, (after_second, ghost_west, ghost_east, flow_all, sea_all))
    return (waves, stokes)
```

```python
import functools
import math

import jax
import jax.numpy as jnp
import numpy as np
from jax import lax
from jax.experimental import pallas as pl
from jax.experimental.pallas import tpu as pltpu
from jax.sharding import PartitionSpec as P

sigma_base = 0.2199
gravity = 9.81
growth = 1.1
courant_scale = 3.0
time_step = 0.5
stokes_gain = 2.0
highest = lax.Precision.HIGHEST
vmem = pl.BlockSpec(memory_space=pltpu.VMEM)
smem = pl.BlockSpec(memory_space=pltpu.SMEM)
params = pltpu.CompilerParams(vmem_limit_bytes=40 * 1024 * 1024)


def tables(freq_count, directions, levels):
    freq_steps = np.arange(freq_count).astype(np.float64)
    radian_freq = sigma_base * growth**freq_steps
    wavenum = radian_freq * radian_freq / gravity
    angles = 2.0 * np.pi * np.arange(directions) / directions
    depths = -(np.arange(levels) + 0.5)
    decays = np.exp(2.0 * wavenum[:, None] * depths[None, :])
    current_weight = decays / np.sum(decays, axis=1, keepdims=True)
    drifts = (radian_freq * wavenum)[:, None] * decays
    drifts = drifts / np.sum(drifts, axis=0, keepdims=True)
    return (angles, current_weight.astype(np.float32), drifts)


def source_kernel(ranks, cores, dir_local, freq_local, blocked, *refs):
    spectra_ref, sea_ref, transfer_ref, gain_ref, damping_ref, out_ref, held = refs
    freq_count = cores * freq_local
    chunks = [
        (
            (s * cores + c) * dir_local * freq_local + d * freq_local,
            (s * dir_local + d) * freq_count + c * freq_local,
        )
        for s in range(ranks)
        for d in range(dir_local)
        for c in range(cores)
    ]
    if blocked:
        for there, here in chunks:
            held[here : here + freq_local, :] = spectra_ref[there : there + freq_local, :]
        spectra = held[...]
    else:
        spectra = spectra_ref[...]
    redist = jnp.dot(
        transfer_ref[...], spectra.astype(jnp.bfloat16), preferred_element_type=jnp.float32
    )
    energy = jnp.sum(spectra * spectra, axis=0, keepdims=True) * (1.0 / spectra.shape[0])
    held[...] = (
        sea_ref[...]
        * (spectra * (1.0 + time_step * gain_ref[...]) + time_step * redist)
        / (1.0 + time_step * damping_ref[...] * energy)
    )
    for there, here in chunks:
        out_ref[there : there + freq_local, :] = held[here : here + freq_local, :]


def sources(spectra, sea_points, transfer, gain, damping, split, blocked):
    return pl.pallas_call(
        functools.partial(source_kernel, *split, blocked),
        out_shape=jax.ShapeDtypeStruct(spectra.shape, jnp.float32),
        in_specs=[vmem] * 5,
        out_specs=vmem,
        scratch_shapes=[pltpu.VMEM(spectra.shape, jnp.float32)],
        compiler_params=params,
        name="sources",
    )(spectra, sea_points, transfer, gain, damping)


def sweep_kernel(rows, dirs, freqs, stride, flow_at, flow_stride, blocked, *refs):
    courant_ref, wave_ref, flow_ref, west_ref, east_ref, sea_ref, out_ref = refs
    columns = wave_ref.shape[-1]
    shape = (rows, columns)
    lane = lax.broadcasted_iota(jnp.int32, shape, 1)
    row = lax.broadcasted_iota(jnp.int32, shape, 0)
    sea = sea_ref[...].astype(jnp.float32)
    first, last = lane == 0, lane == columns - 1
    top, bottom = row == 0, row == rows - 1

    def at_freq(f, carry):
        a = flow_ref[pl.ds(flow_at + f, rows, stride=flow_stride), :]
        b = flow_ref[pl.ds(flow_at + freqs + f, rows, stride=flow_stride), :]
        a_west, a_east = jnp.maximum(a, 0.0), jnp.maximum(-a, 0.0)
        b_north, b_south = jnp.maximum(b, 0.0), jnp.maximum(-b, 0.0)
        for d in range(dirs):
            c = d * freqs + f
            cx, cy = courant_ref[0, c], courant_ref[1, c]
            wave = wave_ref[pl.ds(c, rows, stride=stride), :]
            ghost_west = jnp.where(first, pltpu.roll(west_ref[d], columns - f, 1), 0.0)
            ghost_east = jnp.where(last, pltpu.roll(east_ref[d], columns - 1 - f, 1), 0.0)
            west = jnp.where(first, ghost_west, pltpu.roll(wave, 1, 1))
            east = jnp.where(last, ghost_east, pltpu.roll(wave, columns - 1, 1))
            north = jnp.where(top, 0.0, pltpu.roll(wave, 1, 0))
            south = jnp.where(bottom, 0.0, pltpu.roll(wave, rows - 1, 0))
            moved = (
                wave
                - a_west * (wave - west)
                - a_east * (wave - east)
                - b_north * (wave - north)
                - b_south * (wave - south)
            )
            moved = moved + jnp.maximum(cx, 0.0) * ghost_west + jnp.maximum(-cx, 0.0) * ghost_east
            onward = cx >= 0.0
            speed = jnp.full(shape, jnp.abs(cx), jnp.float32)
            scale = 1.0 / (1.0 + speed)
            ratio = speed * scale
            swept = moved * scale
            place = jnp.where(onward, lane, columns - 1 - lane)
            step = 1
            while step < columns:
                turn = jnp.where(onward, step, columns - step)
                swept = swept + jnp.where(place >= step, ratio, 0.0) * pltpu.roll(swept, turn, 1)
                ratio = ratio * ratio
                step *= 2
            onward = cy >= 0.0
            speed = jnp.full(shape, jnp.abs(cy), jnp.float32)
            scale = 1.0 / (1.0 + speed)
            ratio = speed * scale
            swept = swept * scale
            place = jnp.where(onward, row, rows - 1 - row)
            step = 1
            while step < rows:
                down = pltpu.roll(swept, step, 0)
                up = pltpu.roll(swept, rows - step, 0) if 2 * step != rows else down
                shifted = jnp.where(onward, down, up)
                swept = swept + jnp.where(place >= step, ratio, 0.0) * shifted
                ratio = ratio * ratio
                step *= 2
            if blocked:
                out_ref[pl.ds(c, rows, stride=dirs * freqs), :] = sea * swept
            else:
                out_ref[c] = sea * swept
        return carry

    lax.fori_loop(0, freqs, at_freq, 0)


def neighbour(column, distance):
    devices = range(lax.axis_size("grid"))
    route = [(i - distance, i) for i in devices if i - distance in devices]
    return lax.ppermute(column, "grid", route)


def propagate(wave, flow, flow_at, courant, sea, west_order, east_order, dirs, freqs, blocked):
    rows, held, columns = wave.shape
    comps = dirs * freqs
    edges = (wave[:, :comps, -1], wave[:, :comps, 0])

    def placed(raw, order):
        picked = jnp.take(raw, order, axis=0).reshape(rows, dirs, freqs).transpose(1, 0, 2)
        return jnp.pad(picked, ((0, 0), (0, 0), (0, columns - freqs)))

    west = placed(neighbour(edges[0], 1), west_order)
    east = placed(neighbour(edges[1], -1), east_order)
    shape = (rows * comps, columns) if blocked else (comps, rows, columns)
    return pl.pallas_call(
        functools.partial(
            sweep_kernel, rows, dirs, freqs, held, flow_at, flow.shape[1], blocked
        ),
        out_shape=jax.ShapeDtypeStruct(shape, jnp.float32),
        in_specs=[smem] + [vmem] * 5,
        out_specs=vmem,
        compiler_params=params,
        name="propagate",
    )(courant, wave.reshape(-1, columns), flow.reshape(-1, columns), west, east, sea)


def exchange(payload):
    return lax.all_to_all(payload, ("space", "spec"), split_axis=0, concat_axis=0, tiled=True)


def shards(
    spectrum,
    land_sea,
    west_index,
    east_index,
    current_u,
    current_v,
    transfer,
    wind_rate,
    dissipation,
):
    ranks = lax.axis_size("space")
    cores = lax.axis_size("spec")
    directions, freq_count, rows_local, columns = spectrum.shape[1:]
    levels = current_u.shape[1]
    total_rows = land_sea.shape[1]
    dir_local = directions // ranks
    freq_local = freq_count // cores
    components = directions * freq_count
    comps_local = dir_local * freq_local
    points = rows_local * columns
    groups = ranks * cores
    split = (ranks, cores, dir_local, freq_local)
    space_rank = lax.axis_index("space")
    core_rank = lax.axis_index("spec")
    block_rank = space_rank * cores + core_rank
    angles, current_weight, drifts = tables(freq_count, directions, levels)
    speeds = courant_scale * growth ** (-np.arange(freq_count).astype(np.float64))
    courant = np.stack(
        [np.cos(angles)[:, None] * speeds[None, :], np.sin(angles)[:, None] * speeds[None, :]]
    )
    courant = courant.reshape(2, ranks, dir_local, cores, freq_local).transpose(1, 3, 0, 2, 4)
    courant = courant.reshape(groups, 2, comps_local).astype(np.float32)
    courant = lax.dynamic_index_in_dim(jnp.asarray(courant), block_rank, 0, keepdims=False)

    trig = np.stack([np.cos(angles), np.sin(angles)]) * stokes_gain / math.sqrt(directions)
    stokes_table = trig[:, None, :, None] * drifts.T[None, :, None, :]
    stokes_table = stokes_table.reshape(2 * levels, ranks, dir_local, cores, freq_local)
    stokes_table = stokes_table.transpose(0, 1, 3, 2, 4).reshape(2 * levels, components)
    stokes_table = jnp.asarray(stokes_table.astype(np.float32))

    heading = jnp.asarray((0.5 * (1.0 + np.cos(angles))).astype(np.float32))
    gain = (heading[:, None] * wind_rate[None, :]).reshape(components, 1)
    damping = jnp.broadcast_to(dissipation[None, :], (directions, freq_count))
    damping = damping.reshape(components, 1)
    sea_cells = land_sea[0]
    sea_points = lax.dynamic_slice_in_dim(sea_cells, block_rank * rows_local, rows_local, 0)
    sea_points = sea_points.reshape(1, points).astype(jnp.float32)
    currents = jnp.concatenate(
        [current_u[0].reshape(levels, points), current_v[0].reshape(levels, points)], axis=1
    )
    flow = jnp.dot(jnp.asarray(current_weight), currents, precision=highest)
    flow = flow.reshape(cores, freq_local, 2, points).transpose(0, 2, 1, 3)
    flow = jnp.broadcast_to(
        flow.reshape(1, cores, 2 * freq_local, points), (ranks, cores, 2 * freq_local, points)
    ).reshape(groups, 2 * freq_local, points)

    def by_row(arrived):
        held = arrived.shape[1]
        arrived = arrived.reshape(groups, held, rows_local, columns).transpose(0, 2, 1, 3)
        return arrived.reshape(total_rows, held, columns)

    def step(spectra, blocked):
        return sources(spectra, sea_points, transfer, gain, damping, split, blocked)

    def onward(arrived, flow_part, flow_at, blocked):
        return propagate(
            arrived,
            flow_part,
            flow_at,
            courant,
            sea_cells,
            west_index[0],
            east_index[0],
            dir_local,
            freq_local,
            blocked,
        )

    spectra = step(spectrum[0].reshape(components, points), False)
    blocks = spectra.reshape(groups, comps_local, points)
    first = by_row(exchange(jnp.concatenate([blocks, flow], axis=1)))
    wave = onward(first, first, comps_local, True)
    wave = wave.reshape(groups, rows_local, comps_local, columns).transpose(0, 2, 1, 3)
    returned = exchange(wave.reshape(groups, comps_local, points))
    spectra = step(returned.reshape(components, points), True)
    arrived = by_row(exchange(spectra.reshape(groups, comps_local, points)))
    stokes = jnp.dot(stokes_table, spectra, precision=highest)
    waves = onward(arrived, first, comps_local, False)
    return (
        waves.reshape(1, dir_local, freq_local, total_rows, columns),
        stokes.reshape(1, 2 * levels, rows_local, columns),
    )


def solution(mesh):
    placed = (
        P("grid", None, None, ("space", "spec"), None),
        P("grid", None, None),
        P("grid", None),
        P("grid", None),
        P("grid", None, ("space", "spec"), None),
        P("grid", None, ("space", "spec"), None),
        P(),
        P(),
        P(),
    )
    return jax.shard_map(
        shards,
        mesh=mesh,
        in_specs=placed,
        out_specs=(
            P("grid", "space", "spec", None, None),
            P("grid", None, ("space", "spec"), None),
        ),
        check_vma=False,
    )
```

```python
import functools
import math

import jax
import jax.numpy as jnp
import numpy as np
from jax import lax
from jax.experimental import pallas as pl
from jax.experimental.pallas import tpu as pltpu
from jax.sharding import PartitionSpec as P

sigma_base = 0.2199
gravity = 9.81
growth = 1.1
courant_scale = 3.0
time_step = 0.5
stokes_gain = 2.0
highest = lax.Precision.HIGHEST
mesh_ids = pl.DeviceIdType.MESH
vmem = pl.BlockSpec(memory_space=pltpu.VMEM)
smem = pl.BlockSpec(memory_space=pltpu.SMEM)
anywhere = pl.BlockSpec(memory_space=pl.ANY)


def tables(freq_count, directions, levels):
    freq_steps = np.arange(freq_count).astype(np.float64)
    radian_freq = sigma_base * growth**freq_steps
    wavenum = radian_freq * radian_freq / gravity
    angles = 2.0 * np.pi * np.arange(directions) / directions
    depths = -(np.arange(levels) + 0.5)
    decays = np.exp(2.0 * wavenum[:, None] * depths[None, :])
    current_weight = decays / np.sum(decays, axis=1, keepdims=True)
    drifts = (radian_freq * wavenum)[:, None] * decays
    drifts = drifts / np.sum(drifts, axis=0, keepdims=True)
    return (angles, current_weight.astype(np.float32), drifts)


def wave_kernel(
    ranks,
    cores,
    dirs,
    freqs,
    chunks,
    tile,
    spectrum_ref,
    sea_own_ref,
    sea_ref,
    west_order,
    east_order,
    u_ref,
    v_ref,
    weight_ref,
    gain_ref,
    damping_ref,
    courant_ref,
    transfer_hbm,
    drift_hbm,
    waves_ref,
    stokes_ref,
    transfer_ref,
    drift_ref,
    held,
    flow_send,
    flow_recv,
    flow_x,
    flow_y,
    send,
    recv,
    edge_send,
    west_first,
    east_first,
    west_second,
    east_second,
    order,
    ghosts,
    load_sem,
    send_sem,
    recv_sem,
    flow_send_sem,
    flow_recv_sem,
    edge_send_sem,
    edge_recv_sem,
):
    edge_recv = ((west_first, east_first), (west_second, east_second))
    groups = ranks * cores
    padded = send.shape[2]
    piece = padded // chunks
    rows = recv.shape[1]
    columns = recv.shape[3]
    freq_count = cores * freqs
    plane, planes = lax.axis_index("grid"), lax.axis_size("grid")
    space = lax.axis_index("space")
    me = space * cores + lax.axis_index("spec")
    has_west, has_east = plane > 0, plane < planes - 1
    sides = ((0, has_east, has_west, plane + 1), (1, has_west, has_east, plane - 1))

    def device(level, block):
        return (level, block // cores, block % cores)

    loads = [
        pltpu.make_async_copy(transfer_hbm, transfer_ref, load_sem.at[0]),
        pltpu.make_async_copy(drift_hbm, drift_ref, load_sem.at[1]),
    ]
    for load in loads:
        load.start()

    barrier = pltpu.get_barrier_semaphore()
    for k in range(1, groups):
        partner = device(plane, lax.rem(me + k, groups))
        pl.semaphore_signal(barrier, inc=1, device_id=partner, device_id_type=mesh_ids)
    for _, exists, _, level in sides:

        @pl.when(exists)
        def _():
            for g in range(groups):
                pl.semaphore_signal(
                    barrier, inc=1, device_id=device(level, g), device_id_type=mesh_ids
                )

    def flow_copy(k):
        partner = lax.rem(me + k, groups)
        return pltpu.make_async_remote_copy(
            src_ref=flow_send.at[partner % cores],
            dst_ref=flow_recv.at[me],
            send_sem=flow_send_sem.at[k],
            recv_sem=flow_recv_sem.at[k],
            device_id=device(plane, partner),
            device_id_type=mesh_ids,
        )

    def piece_copy(phase, ch, k):
        partner = lax.rem(me + k, groups)
        part = pl.ds(pl.multiple_of(ch * piece, 8), piece)
        return pltpu.make_async_remote_copy(
            src_ref=send.at[phase, partner, part],
            dst_ref=recv.at[phase, me, part],
            send_sem=send_sem.at[phase, ch, k],
            recv_sem=recv_sem.at[phase, ch, k],
            device_id=device(plane, partner),
            device_id_type=mesh_ids,
        )

    def arrival(phase, ch, k):
        source = lax.rem(me + groups - k, groups)
        part = pl.ds(pl.multiple_of(ch * piece, 8), piece)
        return pltpu.make_async_remote_copy(
            src_ref=send.at[phase, source, part],
            dst_ref=recv.at[phase, source, part],
            send_sem=send_sem.at[phase, ch, k],
            recv_sem=recv_sem.at[phase, ch, k],
            device_id=device(plane, source),
            device_id_type=mesh_ids,
        )

    def edge_copy(stage, side, level, g, rank):
        return pltpu.make_async_remote_copy(
            src_ref=edge_send.at[stage, g],
            dst_ref=edge_recv[stage][side].at[rank],
            send_sem=edge_send_sem.at[stage, side, g],
            recv_sem=edge_recv_sem.at[stage, side, rank],
            device_id=device(level, g),
            device_id_type=mesh_ids,
        )

    for at, current in ((0, u_ref), (1, v_ref)):
        flow = jnp.dot(
            weight_ref[...], current[...], precision=highest, preferred_element_type=jnp.float32
        )
        for c in range(cores):
            flow_send[c, at * freqs : (at + 1) * freqs, :] = flow[c * freqs : (c + 1) * freqs]

    planes_beside = jnp.minimum(plane, 1) + jnp.minimum(planes - 1 - plane, 1)
    pl.semaphore_wait(barrier, groups - 1 + groups * planes_beside)

    for k in range(1, groups):
        flow_copy(k).start()
    flow_recv[me] = flow_send[lax.axis_index("spec")]

    natural = [
        (s * cores + c, d, (s * dirs + d) * freq_count + c * freqs)
        for s in range(ranks)
        for d in range(dirs)
        for c in range(cores)
    ]
    lane8 = lax.broadcasted_iota(jnp.int32, (8, columns), 1)
    row8 = lax.broadcasted_iota(jnp.int32, (8, columns), 0)
    ends = (row8 == 0) & (lane8 == columns - 1) | (row8 == 1) & (lane8 == 0)
    ends = ends.astype(jnp.float32)

    def sources(stage, spectra):
        phase = 2 * stage
        redist = jnp.dot(
            transfer_ref[...], spectra.astype(jnp.bfloat16), preferred_element_type=jnp.float32
        )
        energy = jnp.sum(spectra * spectra, axis=0, keepdims=True) * (1.0 / spectra.shape[0])
        held[...] = (
            sea_own_ref[...]
            * (spectra * (1.0 + time_step * gain_ref[...]) + time_step * redist)
            / (1.0 + time_step * damping_ref[...] * energy)
        )
        for g, d, here in natural:
            send[phase, g, pl.ds(d, freqs, stride=dirs), :] = held[here : here + freqs, :]
        for k in range(1, groups):
            piece_copy(phase, 0, k).start()
        for g in range(groups):
            edge_send[stage, g, :, :padded] = lax.dot_general(
                ends,
                send[phase, g],
                (((1,), (1,)), ((), ())),
                precision=highest,
                preferred_element_type=jnp.float32,
            )
        for side, exists, _, level in sides:

            @pl.when(exists)
            def _():
                for g in range(groups):
                    edge_copy(stage, side, level, g, me).start()

        for ch in range(1, chunks):
            for k in range(1, groups):
                piece_copy(phase, ch, k).start()
        recv[phase, me] = send[phase, me]

    def border(stage):
        for side, _, exists, level in sides:
            wanted = (west_order, east_order)[side]

            @pl.when(exists)
            def _():
                for r in range(groups):
                    edge_copy(stage, side, level, r, r).wait_recv()
                order[...] = jnp.zeros_like(order)
                for y in range(rows):
                    order[y : y + 1, :] = edge_recv[stage][side][wanted[y], side : side + 1, :]
                square = (padded, padded)
                unit = lax.broadcasted_iota(jnp.int32, square, 0) == lax.broadcasted_iota(
                    jnp.int32, square, 1
                )
                ghosts[side] = lax.dot_general(
                    unit.astype(jnp.float32),
                    order[:, :padded],
                    (((1,), (1,)), ((), ())),
                    precision=highest,
                    preferred_element_type=jnp.float32,
                )

            @pl.when(jnp.logical_not(exists))
            def _():
                ghosts[side] = jnp.zeros(ghosts.shape[1:], jnp.float32)

    shape = (tile, columns)
    lane = lax.broadcasted_iota(jnp.int32, shape, 1)
    first, last = lane == 0, lane == columns - 1
    quadrant = (space * dirs) // (ranks * dirs // 4)
    onward = (quadrant == 0) | (quadrant == 3)
    ahead = onward.astype(jnp.int32)
    place = ahead * lane + (1 - ahead) * (columns - 1 - lane)

    def rolled(block, turn):
        flat = pltpu.roll(block.reshape(-1, columns), turn, 1)
        return flat.reshape(block.shape)

    def sweep(phase, base):
        part = pl.ds(pl.multiple_of(base, 8), tile)
        wave = recv[phase, :, part, :]
        a, b = flow_x[:, part, :], flow_y[:, part, :]
        cx = jnp.broadcast_to(courant_ref[0, part, :], shape)
        cy = jnp.broadcast_to(courant_ref[1, part, :], shape)
        raw_west, raw_east = ghosts[0, part, :], ghosts[1, part, :]
        ghost_west = jnp.stack(
            [
                jnp.where(first, pltpu.roll(raw_west, (columns - y) % columns, 1), 0.0)
                for y in range(rows)
            ]
        )
        ghost_east = jnp.stack(
            [
                jnp.where(last, pltpu.roll(raw_east, columns - 1 - y, 1), 0.0)
                for y in range(rows)
            ]
        )
        blank = jnp.zeros((1,) + shape, jnp.float32)
        west = jnp.where(first[None], ghost_west, rolled(wave, 1))
        east = jnp.where(last[None], ghost_east, rolled(wave, columns - 1))
        north = jnp.concatenate([blank, wave[:-1]], axis=0)
        south = jnp.concatenate([wave[1:], blank], axis=0)
        moved = (
            wave
            - jnp.maximum(a, 0.0) * (wave - west)
            - jnp.maximum(-a, 0.0) * (wave - east)
            - jnp.maximum(b, 0.0) * (wave - north)
            - jnp.maximum(-b, 0.0) * (wave - south)
            + jnp.maximum(cx, 0.0)[None] * ghost_west
            + jnp.maximum(-cx, 0.0)[None] * ghost_east
        )
        speed = jnp.abs(cx)
        scale = 1.0 / (1.0 + speed)
        ratio = speed * scale
        swept = moved * scale[None]
        step = 1
        while step < columns:
            turn = ahead * step + (1 - ahead) * (columns - step)
            swept = swept + jnp.where(place >= step, ratio, 0.0)[None] * rolled(swept, turn)
            ratio = ratio * ratio
            step *= 2
        scale = 1.0 / (1.0 + jnp.abs(cy))
        down, up = jnp.maximum(cy, 0.0) * scale, jnp.maximum(-cy, 0.0) * scale
        lines = [swept[y] * scale for y in range(rows)]
        for y in range(1, rows):
            lines[y] = lines[y] + down * lines[y - 1]
        for y in range(rows - 2, -1, -1):
            lines[y] = lines[y] + up * lines[y + 1]
        return [sea_ref[y : y + 1, :].astype(jnp.float32) * lines[y] for y in range(rows)]

    def propagate(phase, emit, after):
        def chunk(ch, carry):
            for k in range(1, groups):
                arrival(phase, ch, k).wait_recv()
            for t in range(piece // tile):
                base = ch * piece + t * tile
                emit(base, sweep(phase, base))
            after(ch)
            return carry

        lax.fori_loop(0, chunks, chunk, 0)

    def emit_send(base, lines):
        for y in range(rows):
            send[1, y, pl.ds(pl.multiple_of(base, 8), tile), :] = lines[y]

    def send_piece(ch):
        for k in range(1, groups):
            piece_copy(1, ch, k).start()
        part = pl.ds(pl.multiple_of(ch * piece, 8), piece)
        recv[1, me, part, :] = send[1, me, part, :]

    def emit_waves(base, lines):
        freq = base // dirs
        for y in range(rows):
            for f in range(min(tile // dirs, freqs)):
                waves_ref[pl.ds((freq + f) * rows + y, dirs, stride=freqs * rows), :] = lines[y][
                    f * dirs : (f + 1) * dirs
                ]

    loads[0].wait()
    sources(0, spectrum_ref[...])
    for k in range(1, groups):
        source = lax.rem(me + groups - k, groups)
        pltpu.make_async_remote_copy(
            src_ref=flow_send.at[0],
            dst_ref=flow_recv.at[source],
            send_sem=flow_send_sem.at[k],
            recv_sem=flow_recv_sem.at[k],
            device_id=device(plane, source),
            device_id_type=mesh_ids,
        ).wait_recv()
    for f in range(freqs):
        wide = (rows, dirs, columns)
        flow_x[:, f * dirs : (f + 1) * dirs, :] = jnp.broadcast_to(
            flow_recv[:, f : f + 1, :], wide
        )
        flow_y[:, f * dirs : (f + 1) * dirs, :] = jnp.broadcast_to(
            flow_recv[:, freqs + f : freqs + f + 1, :], wide
        )
    border(0)
    propagate(0, emit_send, send_piece)
    for k in range(1, groups):
        for ch in range(chunks):
            arrival(1, ch, k).wait_recv()
    for g, d, here in natural:
        held[here : here + freqs, :] = recv[1, g, pl.ds(d, freqs, stride=dirs), :]
    sources(1, held[...])
    loads[1].wait()
    stokes_ref[...] = jnp.dot(
        drift_ref[...], held[...], precision=highest, preferred_element_type=jnp.float32
    )
    border(1)
    propagate(2, emit_waves, lambda ch: None)

    for k in range(1, groups):
        flow_copy(k).wait_send()
        for phase in range(3):
            for ch in range(chunks):
                piece_copy(phase, ch, k).wait_send()
    for stage in range(2):
        for side, exists, _, level in sides:

            @pl.when(exists)
            def _():
                for g in range(groups):
                    edge_copy(stage, side, level, g, me).wait_send()


def rounded_up(count, unit):
    return -(-count // unit) * unit


def shards(
    spectrum,
    land_sea,
    west_index,
    east_index,
    current_u,
    current_v,
    transfer,
    wind_rate,
    dissipation,
):
    ranks = lax.axis_size("space")
    cores = lax.axis_size("spec")
    directions, freq_count, rows_local, columns = spectrum.shape[1:]
    levels = current_u.shape[1]
    total_rows = land_sea.shape[1]
    dir_local = directions // ranks
    freq_local = freq_count // cores
    components = directions * freq_count
    comps_local = dir_local * freq_local
    groups = ranks * cores
    padded = rounded_up(comps_local, 8)
    tile = 24 if padded % 24 == 0 else 8
    chunks = 3 if padded % (3 * tile) == 0 else 1
    width = rounded_up(padded, 128)
    flow_rows = rounded_up(2 * freq_local, 8)
    space_rank = lax.axis_index("space")
    core_rank = lax.axis_index("spec")
    block_rank = space_rank * cores + core_rank
    angles, current_weight, drifts = tables(freq_count, directions, levels)
    cosines, sines = np.cos(angles), np.sin(angles)
    cosines[np.abs(cosines) < 1e-12] = 0.0
    sines[np.abs(sines) < 1e-12] = 0.0
    speeds = courant_scale * growth ** (-np.arange(freq_count).astype(np.float64))
    courant = np.stack([cosines[:, None] * speeds[None, :], sines[:, None] * speeds[None, :]])
    courant = courant.reshape(2, ranks, dir_local, cores, freq_local).transpose(1, 3, 0, 4, 2)
    courant = courant.reshape(groups, 2, comps_local, 1).astype(np.float32)
    courant = np.pad(courant, ((0, 0), (0, 0), (0, padded - comps_local), (0, 0)))
    courant = lax.dynamic_index_in_dim(jnp.asarray(courant), block_rank, 0, keepdims=False)

    trig = np.stack([cosines, sines]) * stokes_gain / math.sqrt(directions)
    stokes_table = trig[:, None, :, None] * drifts.T[None, :, None, :]
    stokes_table = stokes_table.reshape(2 * levels, components).astype(np.float32)

    heading = jnp.asarray((0.5 * (1.0 + cosines)).astype(np.float32))
    gain = (heading[:, None] * wind_rate[None, :]).reshape(components, 1)
    damping = jnp.broadcast_to(dissipation[None, :], (directions, freq_count))
    damping = damping.reshape(components, 1)
    sea_own = lax.dynamic_slice_in_dim(land_sea[0], block_rank, 1, 0).astype(jnp.float32)
    f32 = jnp.float32
    waves, stokes = pl.pallas_call(
        functools.partial(
            wave_kernel, ranks, cores, dir_local, freq_local, chunks, tile
        ),
        out_shape=(
            jax.ShapeDtypeStruct((comps_local * total_rows, columns), f32),
            jax.ShapeDtypeStruct((2 * levels, columns), f32),
        ),
        in_specs=[vmem] * 3 + [smem] * 2 + [vmem] * 6 + [anywhere] * 2,
        out_specs=(vmem, vmem),
        scratch_shapes=[
            pltpu.VMEM(transfer.shape, transfer.dtype),
            pltpu.VMEM(stokes_table.shape, f32),
            pltpu.VMEM((components, columns), f32),
            pltpu.VMEM((cores, flow_rows, columns), f32),
            pltpu.VMEM((groups, flow_rows, columns), f32),
            pltpu.VMEM((groups, padded, columns), f32),
            pltpu.VMEM((groups, padded, columns), f32),
            pltpu.VMEM((3, groups, padded, columns), f32),
            pltpu.VMEM((3, groups, padded, columns), f32),
            pltpu.VMEM((2, groups, 8, width), f32),
            pltpu.VMEM((groups, 8, width), f32),
            pltpu.VMEM((groups, 8, width), f32),
            pltpu.VMEM((groups, 8, width), f32),
            pltpu.VMEM((groups, 8, width), f32),
            pltpu.VMEM((columns, width), f32),
            pltpu.VMEM((2, padded, columns), f32),
            pltpu.SemaphoreType.DMA((2,)),
            pltpu.SemaphoreType.DMA((3, chunks, groups)),
            pltpu.SemaphoreType.DMA((3, chunks, groups)),
            pltpu.SemaphoreType.DMA((groups,)),
            pltpu.SemaphoreType.DMA((groups,)),
            pltpu.SemaphoreType.DMA((2, 2, groups)),
            pltpu.SemaphoreType.DMA((2, 2, groups)),
        ],
        compiler_params=pltpu.CompilerParams(
            collective_id=0, has_side_effects=True, vmem_limit_bytes=48 * 1024 * 1024
        ),
        name="waves",
    )(
        spectrum[0].reshape(components, columns),
        sea_own,
        land_sea[0],
        west_index[0],
        east_index[0],
        current_u[0].reshape(levels, columns),
        current_v[0].reshape(levels, columns),
        jnp.asarray(current_weight),
        gain,
        damping,
        courant,
        transfer,
        jnp.asarray(stokes_table),
    )
    return (
        waves.reshape(1, dir_local, freq_local, total_rows, columns),
        stokes.reshape(1, 2 * levels, rows_local, columns),
    )


def solution(mesh):
    placed = (
        P("grid", None, None, ("space", "spec"), None),
        P("grid", None, None),
        P("grid", None),
        P("grid", None),
        P("grid", None, ("space", "spec"), None),
        P("grid", None, ("space", "spec"), None),
        P(),
        P(),
        P(),
    )
    return jax.shard_map(
        shards,
        mesh=mesh,
        in_specs=placed,
        out_specs=(
            P("grid", "space", "spec", None, None),
            P("grid", None, ("space", "spec"), None),
        ),
        check_vma=False,
    )
```

```python
import functools
import math

import jax
import jax.numpy as jnp
import numpy as np
from jax import lax
from jax.experimental import pallas as pl
from jax.experimental.pallas import tpu as pltpu
from jax.sharding import PartitionSpec as P

sigma_base = 0.2199
gravity = 9.81
growth = 1.1
courant_scale = 3.0
time_step = 0.5
stokes_gain = 2.0
highest = lax.Precision.HIGHEST
mesh_ids = pl.DeviceIdType.MESH
vmem = pl.BlockSpec(memory_space=pltpu.VMEM)
in_place = pl.BlockSpec(memory_space=pltpu.HBM)


def tables(freq_count, directions, levels):
    freq_steps = np.arange(freq_count).astype(np.float64)
    radian_freq = sigma_base * growth**freq_steps
    wavenum = radian_freq * radian_freq / gravity
    angles = 2.0 * np.pi * np.arange(directions) / directions
    depths = -(np.arange(levels) + 0.5)
    decays = np.exp(2.0 * wavenum[:, None] * depths[None, :])
    current_weight = decays / np.sum(decays, axis=1, keepdims=True)
    drifts = (radian_freq * wavenum)[:, None] * decays
    drifts = drifts / np.sum(drifts, axis=0, keepdims=True)
    return (angles, current_weight.astype(np.float32), drifts)


def wave_kernel(
    ranks,
    cores,
    dirs,
    freqs,
    chunks,
    tile,
    u_hbm,
    v_hbm,
    weight_hbm,
    wind_hbm,
    dissipation_hbm,
    spread_hbm,
    spectrum_hbm,
    transfer_hbm,
    sea_hbm,
    courant_hbm,
    west_hbm,
    east_hbm,
    drift_hbm,
    waves_ref,
    stokes_ref,
    u_ref,
    v_ref,
    weight_ref,
    wind_ref,
    dissipation_ref,
    spread_ref,
    spectrum_ref,
    transfer_ref,
    sea_ref,
    courant_ref,
    west_order,
    east_order,
    drift_ref,
    gain_ref,
    damping_ref,
    held,
    flow_send,
    flow_recv,
    flow_x,
    flow_y,
    send,
    recv,
    edge_send,
    west_first,
    east_first,
    west_second,
    east_second,
    order,
    ghosts,
    load_sem,
    send_sem,
    recv_sem,
    flow_send_sem,
    flow_recv_sem,
    edge_send_sem,
    edge_recv_sem,
):
    edge_recv = ((west_first, east_first), (west_second, east_second))
    groups = ranks * cores
    padded = send.shape[2]
    piece = padded // chunks
    rows = recv.shape[1]
    columns = recv.shape[3]
    freq_count = cores * freqs
    plane, planes = lax.axis_index("grid"), lax.axis_size("grid")
    space = lax.axis_index("space")
    me = space * cores + lax.axis_index("spec")
    has_west, has_east = plane > 0, plane < planes - 1
    sides = ((0, has_east, has_west, plane + 1), (1, has_west, has_east, plane - 1))

    def device(level, block):
        return (level, block // cores, block % cores)

    barrier = pltpu.get_barrier_semaphore()
    for k in range(1, groups):
        partner = device(plane, lax.rem(me + k, groups))
        pl.semaphore_signal(barrier, inc=1, device_id=partner, device_id_type=mesh_ids)
    for _, exists, _, level in sides:

        @pl.when(exists)
        def _():
            for g in range(groups):
                pl.semaphore_signal(
                    barrier, inc=1, device_id=device(level, g), device_id_type=mesh_ids
                )

    loads = [
        pltpu.make_async_copy(source, target, load_sem.at[i])
        for i, (source, target) in enumerate(
            (
                (u_hbm, u_ref),
                (v_hbm, v_ref),
                (weight_hbm, weight_ref),
                (wind_hbm, wind_ref),
                (dissipation_hbm, dissipation_ref),
                (spread_hbm, spread_ref),
                (spectrum_hbm, spectrum_ref),
                (transfer_hbm, transfer_ref),
                (sea_hbm, sea_ref),
                (courant_hbm.at[me], courant_ref),
                (west_hbm, west_order),
                (east_hbm, east_order),
                (drift_hbm, drift_ref),
            )
        )
    ]
    for load in loads:
        load.start()

    def flow_copy(k):
        partner = lax.rem(me + k, groups)
        return pltpu.make_async_remote_copy(
            src_ref=flow_send.at[partner % cores],
            dst_ref=flow_recv.at[me],
            send_sem=flow_send_sem.at[k],
            recv_sem=flow_recv_sem.at[k],
            device_id=device(plane, partner),
            device_id_type=mesh_ids,
        )

    def piece_copy(phase, ch, k):
        partner = lax.rem(me + k, groups)
        part = pl.ds(pl.multiple_of(ch * piece, 8), piece)
        return pltpu.make_async_remote_copy(
            src_ref=send.at[phase, partner, part],
            dst_ref=recv.at[phase, me, part],
            send_sem=send_sem.at[phase, ch, k],
            recv_sem=recv_sem.at[phase, ch, k],
            device_id=device(plane, partner),
            device_id_type=mesh_ids,
        )

    def arrival(phase, ch, k):
        source = lax.rem(me + groups - k, groups)
        part = pl.ds(pl.multiple_of(ch * piece, 8), piece)
        return pltpu.make_async_remote_copy(
            src_ref=send.at[phase, source, part],
            dst_ref=recv.at[phase, source, part],
            send_sem=send_sem.at[phase, ch, k],
            recv_sem=recv_sem.at[phase, ch, k],
            device_id=device(plane, source),
            device_id_type=mesh_ids,
        )

    def edge_copy(stage, side, level, g, rank):
        return pltpu.make_async_remote_copy(
            src_ref=edge_send.at[stage, g],
            dst_ref=edge_recv[stage][side].at[rank],
            send_sem=edge_send_sem.at[stage, side, g],
            recv_sem=edge_recv_sem.at[stage, side, rank],
            device_id=device(level, g),
            device_id_type=mesh_ids,
        )

    for load in loads[:6]:
        load.wait()
    for at, current in ((0, u_ref), (1, v_ref)):
        flow = jnp.dot(
            weight_ref[...], current[...], precision=highest, preferred_element_type=jnp.float32
        )
        for c in range(cores):
            flow_send[c, at * freqs : (at + 1) * freqs, :] = flow[c * freqs : (c + 1) * freqs]

    for at, rate, factor in ((0, wind_ref, gain_ref), (1, dissipation_ref, damping_ref)):
        factor[...] = lax.dot_general(
            spread_ref[at],
            jnp.broadcast_to(rate[...], (columns, freq_count)),
            (((1,), (1,)), ((), ())),
            precision=highest,
            preferred_element_type=jnp.float32,
        )

    planes_beside = jnp.minimum(plane, 1) + jnp.minimum(planes - 1 - plane, 1)
    pl.semaphore_wait(barrier, groups - 1 + groups * planes_beside)

    for k in range(1, groups):
        flow_copy(k).start()
    flow_recv[me] = flow_send[lax.axis_index("spec")]

    natural = [
        (s * cores + c, d, (s * dirs + d) * freq_count + c * freqs)
        for s in range(ranks)
        for d in range(dirs)
        for c in range(cores)
    ]
    lane8 = lax.broadcasted_iota(jnp.int32, (8, columns), 1)
    row8 = lax.broadcasted_iota(jnp.int32, (8, columns), 0)
    ends = (row8 == 0) & (lane8 == columns - 1) | (row8 == 1) & (lane8 == 0)
    ends = ends.astype(jnp.float32)

    def sources(stage, spectra):
        phase = 2 * stage
        redist = jnp.dot(
            transfer_ref[...], spectra.astype(jnp.bfloat16), preferred_element_type=jnp.float32
        )
        energy = jnp.sum(spectra * spectra, axis=0, keepdims=True) * (1.0 / spectra.shape[0])
        held[...] = (
            sea_ref[pl.ds(me, 1), :].astype(jnp.float32)
            * (spectra * (1.0 + time_step * gain_ref[...]) + time_step * redist)
            / (1.0 + time_step * damping_ref[...] * energy)
        )
        for g, d, here in natural:
            send[phase, g, pl.ds(d, freqs, stride=dirs), :] = held[here : here + freqs, :]
        for k in range(1, groups):
            piece_copy(phase, 0, k).start()
        for g in range(groups):
            edge_send[stage, g, :, :padded] = lax.dot_general(
                ends,
                send[phase, g],
                (((1,), (1,)), ((), ())),
                precision=highest,
                preferred_element_type=jnp.float32,
            )
        for side, exists, _, level in sides:

            @pl.when(exists)
            def _():
                for g in range(groups):
                    edge_copy(stage, side, level, g, me).start()

        for ch in range(1, chunks):
            for k in range(1, groups):
                piece_copy(phase, ch, k).start()
        recv[phase, me] = send[phase, me]

    def border(stage):
        for side, _, exists, level in sides:
            wanted = (west_order, east_order)[side]

            @pl.when(exists)
            def _():
                for r in range(groups):
                    edge_copy(stage, side, level, r, r).wait_recv()
                order[...] = jnp.zeros_like(order)
                for y in range(rows):
                    order[y : y + 1, :] = edge_recv[stage][side][wanted[0, y], side : side + 1, :]
                square = (padded, padded)
                unit = lax.broadcasted_iota(jnp.int32, square, 0) == lax.broadcasted_iota(
                    jnp.int32, square, 1
                )
                ghosts[side] = lax.dot_general(
                    unit.astype(jnp.float32),
                    order[:, :padded],
                    (((1,), (1,)), ((), ())),
                    precision=highest,
                    preferred_element_type=jnp.float32,
                )

            @pl.when(jnp.logical_not(exists))
            def _():
                ghosts[side] = jnp.zeros(ghosts.shape[1:], jnp.float32)

    shape = (tile, columns)
    lane = lax.broadcasted_iota(jnp.int32, shape, 1)
    first, last = lane == 0, lane == columns - 1
    quadrant = (space * dirs) // (ranks * dirs // 4)
    onward = (quadrant == 0) | (quadrant == 3)
    ahead = onward.astype(jnp.int32)
    place = ahead * lane + (1 - ahead) * (columns - 1 - lane)

    def rolled(block, turn):
        flat = pltpu.roll(block.reshape(-1, columns), turn, 1)
        return flat.reshape(block.shape)

    def sweep(phase, base):
        part = pl.ds(pl.multiple_of(base, 8), tile)
        wave = recv[phase, :, part, :]
        a, b = flow_x[:, part, :], flow_y[:, part, :]
        cx = jnp.broadcast_to(courant_ref[0, part, :], shape)
        cy = jnp.broadcast_to(courant_ref[1, part, :], shape)
        raw_west, raw_east = ghosts[0, part, :], ghosts[1, part, :]
        ghost_west = jnp.stack(
            [
                jnp.where(first, pltpu.roll(raw_west, (columns - y) % columns, 1), 0.0)
                for y in range(rows)
            ]
        )
        ghost_east = jnp.stack(
            [
                jnp.where(last, pltpu.roll(raw_east, columns - 1 - y, 1), 0.0)
                for y in range(rows)
            ]
        )
        blank = jnp.zeros((1,) + shape, jnp.float32)
        west = jnp.where(first[None], ghost_west, rolled(wave, 1))
        east = jnp.where(last[None], ghost_east, rolled(wave, columns - 1))
        north = jnp.concatenate([blank, wave[:-1]], axis=0)
        south = jnp.concatenate([wave[1:], blank], axis=0)
        moved = (
            wave
            - jnp.maximum(a, 0.0) * (wave - west)
            - jnp.maximum(-a, 0.0) * (wave - east)
            - jnp.maximum(b, 0.0) * (wave - north)
            - jnp.maximum(-b, 0.0) * (wave - south)
            + jnp.maximum(cx, 0.0)[None] * ghost_west
            + jnp.maximum(-cx, 0.0)[None] * ghost_east
        )
        speed = jnp.abs(cx)
        scale = 1.0 / (1.0 + speed)
        ratio = speed * scale
        swept = moved * scale[None]
        step = 1
        while step < columns:
            turn = ahead * step + (1 - ahead) * (columns - step)
            swept = swept + jnp.where(place >= step, ratio, 0.0)[None] * rolled(swept, turn)
            ratio = ratio * ratio
            step *= 2
        scale = 1.0 / (1.0 + jnp.abs(cy))
        down, up = jnp.maximum(cy, 0.0) * scale, jnp.maximum(-cy, 0.0) * scale
        lines = [swept[y] * scale for y in range(rows)]
        for y in range(1, rows):
            lines[y] = lines[y] + down * lines[y - 1]
        for y in range(rows - 2, -1, -1):
            lines[y] = lines[y] + up * lines[y + 1]
        return [sea_ref[y : y + 1, :].astype(jnp.float32) * lines[y] for y in range(rows)]

    def propagate(phase, emit, after):
        def chunk(ch, carry):
            for k in range(1, groups):
                arrival(phase, ch, k).wait_recv()
            for t in range(piece // tile):
                base = ch * piece + t * tile
                emit(base, sweep(phase, base))
            after(ch)
            return carry

        lax.fori_loop(0, chunks, chunk, 0)

    def emit_send(base, lines):
        for y in range(rows):
            send[1, y, pl.ds(pl.multiple_of(base, 8), tile), :] = lines[y]

    def send_piece(ch):
        for k in range(1, groups):
            piece_copy(1, ch, k).start()
        part = pl.ds(pl.multiple_of(ch * piece, 8), piece)
        recv[1, me, part, :] = send[1, me, part, :]

    def emit_waves(base, lines):
        freq = base // dirs
        for y in range(rows):
            for f in range(min(tile // dirs, freqs)):
                waves_ref[pl.ds((freq + f) * rows + y, dirs, stride=freqs * rows), :] = lines[y][
                    f * dirs : (f + 1) * dirs
                ]

    for load in loads[6:-1]:
        load.wait()
    sources(0, spectrum_ref[...])
    for k in range(1, groups):
        source = lax.rem(me + groups - k, groups)
        pltpu.make_async_remote_copy(
            src_ref=flow_send.at[0],
            dst_ref=flow_recv.at[source],
            send_sem=flow_send_sem.at[k],
            recv_sem=flow_recv_sem.at[k],
            device_id=device(plane, source),
            device_id_type=mesh_ids,
        ).wait_recv()
    for f in range(freqs):
        wide = (rows, dirs, columns)
        flow_x[:, f * dirs : (f + 1) * dirs, :] = jnp.broadcast_to(
            flow_recv[:, f : f + 1, :], wide
        )
        flow_y[:, f * dirs : (f + 1) * dirs, :] = jnp.broadcast_to(
            flow_recv[:, freqs + f : freqs + f + 1, :], wide
        )
    border(0)
    propagate(0, emit_send, send_piece)
    for k in range(1, groups):
        for ch in range(chunks):
            arrival(1, ch, k).wait_recv()
    for g, d, here in natural:
        held[here : here + freqs, :] = recv[1, g, pl.ds(d, freqs, stride=dirs), :]
    sources(1, held[...])
    loads[-1].wait()
    stokes_ref[...] = jnp.dot(
        drift_ref[...], held[...], precision=highest, preferred_element_type=jnp.float32
    )
    border(1)
    propagate(2, emit_waves, lambda ch: None)

    for k in range(1, groups):
        flow_copy(k).wait_send()
        for phase in range(3):
            for ch in range(chunks):
                piece_copy(phase, ch, k).wait_send()
    for stage in range(2):
        for side, exists, _, level in sides:

            @pl.when(exists)
            def _():
                for g in range(groups):
                    edge_copy(stage, side, level, g, me).wait_send()


def rounded_up(count, unit):
    return -(-count // unit) * unit


def shards(
    spectrum,
    land_sea,
    west_index,
    east_index,
    current_u,
    current_v,
    transfer,
    wind_rate,
    dissipation,
):
    ranks = lax.axis_size("space")
    cores = lax.axis_size("spec")
    directions, freq_count, rows_local, columns = spectrum.shape[1:]
    levels = current_u.shape[1]
    total_rows = land_sea.shape[1]
    dir_local = directions // ranks
    freq_local = freq_count // cores
    components = directions * freq_count
    comps_local = dir_local * freq_local
    groups = ranks * cores
    padded = rounded_up(comps_local, 8)
    tile = 24 if padded % 24 == 0 else 8
    chunks = 3 if padded % (3 * tile) == 0 else 1
    width = rounded_up(padded, 128)
    flow_rows = rounded_up(2 * freq_local, 8)
    angles, current_weight, drifts = tables(freq_count, directions, levels)
    cosines, sines = np.cos(angles), np.sin(angles)
    cosines[np.abs(cosines) < 1e-12] = 0.0
    sines[np.abs(sines) < 1e-12] = 0.0
    speeds = courant_scale * growth ** (-np.arange(freq_count).astype(np.float64))
    courant = np.stack([cosines[:, None] * speeds[None, :], sines[:, None] * speeds[None, :]])
    courant = courant.reshape(2, ranks, dir_local, cores, freq_local).transpose(1, 3, 0, 4, 2)
    courant = courant.reshape(groups, 2, comps_local, 1).astype(np.float32)
    courant = np.pad(courant, ((0, 0), (0, 0), (0, padded - comps_local), (0, 0)))

    trig = np.stack([cosines, sines]) * stokes_gain / math.sqrt(directions)
    stokes_table = trig[:, None, :, None] * drifts.T[None, :, None, :]
    stokes_table = stokes_table.reshape(2 * levels, components).astype(np.float32)

    heading = np.repeat(0.5 * (1.0 + cosines), freq_count)[:, None]
    unit = np.tile(np.eye(freq_count), (directions, 1))
    spread = np.stack([heading * unit, unit]).astype(np.float32)
    f32 = jnp.float32
    waves, stokes = pl.pallas_call(
        functools.partial(
            wave_kernel, ranks, cores, dir_local, freq_local, chunks, tile
        ),
        out_shape=(
            jax.ShapeDtypeStruct((comps_local * total_rows, columns), f32),
            jax.ShapeDtypeStruct((2 * levels, columns), f32),
        ),
        in_specs=[in_place] * 13,
        out_specs=(vmem, vmem),
        scratch_shapes=[
            pltpu.VMEM((levels, columns), f32),
            pltpu.VMEM((levels, columns), f32),
            pltpu.VMEM(current_weight.shape, f32),
            pltpu.VMEM((1, freq_count), f32),
            pltpu.VMEM((1, freq_count), f32),
            pltpu.VMEM(spread.shape, f32),
            pltpu.VMEM((components, columns), f32),
            pltpu.VMEM(transfer.shape, transfer.dtype),
            pltpu.VMEM(land_sea.shape[1:], land_sea.dtype),
            pltpu.VMEM(courant.shape[1:], f32),
            pltpu.SMEM(west_index.shape, west_index.dtype),
            pltpu.SMEM(east_index.shape, east_index.dtype),
            pltpu.VMEM(stokes_table.shape, f32),
            pltpu.VMEM((components, columns), f32),
            pltpu.VMEM((components, columns), f32),
            pltpu.VMEM((components, columns), f32),
            pltpu.VMEM((cores, flow_rows, columns), f32),
            pltpu.VMEM((groups, flow_rows, columns), f32),
            pltpu.VMEM((groups, padded, columns), f32),
            pltpu.VMEM((groups, padded, columns), f32),
            pltpu.VMEM((3, groups, padded, columns), f32),
            pltpu.VMEM((3, groups, padded, columns), f32),
            pltpu.VMEM((2, groups, 8, width), f32),
            pltpu.VMEM((groups, 8, width), f32),
            pltpu.VMEM((groups, 8, width), f32),
            pltpu.VMEM((groups, 8, width), f32),
            pltpu.VMEM((groups, 8, width), f32),
            pltpu.VMEM((columns, width), f32),
            pltpu.VMEM((2, padded, columns), f32),
            pltpu.SemaphoreType.DMA((13,)),
            pltpu.SemaphoreType.DMA((3, chunks, groups)),
            pltpu.SemaphoreType.DMA((3, chunks, groups)),
            pltpu.SemaphoreType.DMA((groups,)),
            pltpu.SemaphoreType.DMA((groups,)),
            pltpu.SemaphoreType.DMA((2, 2, groups)),
            pltpu.SemaphoreType.DMA((2, 2, groups)),
        ],
        compiler_params=pltpu.CompilerParams(
            collective_id=0, has_side_effects=True, vmem_limit_bytes=40 * 1024 * 1024
        ),
        name="waves",
    )(
        current_u[0].reshape(levels, columns),
        current_v[0].reshape(levels, columns),
        jnp.asarray(current_weight),
        wind_rate.reshape(1, freq_count),
        dissipation.reshape(1, freq_count),
        jnp.asarray(spread),
        spectrum[0].reshape(components, columns),
        transfer,
        land_sea[0],
        jnp.asarray(courant),
        west_index,
        east_index,
        jnp.asarray(stokes_table),
    )
    return (
        waves.reshape(1, dir_local, freq_local, total_rows, columns),
        stokes.reshape(1, 2 * levels, rows_local, columns),
    )


def solution(mesh):
    placed = (
        P("grid", None, None, ("space", "spec"), None),
        P("grid", None, None),
        P("grid", None),
        P("grid", None),
        P("grid", None, ("space", "spec"), None),
        P("grid", None, ("space", "spec"), None),
        P(),
        P(),
        P(),
    )
    return jax.shard_map(
        shards,
        mesh=mesh,
        in_specs=placed,
        out_specs=(
            P("grid", "space", "spec", None, None),
            P("grid", None, ("space", "spec"), None),
        ),
        check_vma=False,
    )
```

```python
import functools
import math

import jax
import jax.numpy as jnp
import numpy as np
from jax import lax
from jax.experimental import pallas as pl
from jax.experimental.pallas import tpu as pltpu
from jax.sharding import PartitionSpec as P

sigma_base = 0.2199
gravity = 9.81
growth = 1.1
courant_scale = 3.0
time_step = 0.5
stokes_gain = 2.0
highest = lax.Precision.HIGHEST
mesh_ids = pl.DeviceIdType.MESH
in_place = pl.BlockSpec(memory_space=pltpu.HBM)


def tables(freq_count, directions, levels):
    freq_steps = np.arange(freq_count).astype(np.float64)
    radian_freq = sigma_base * growth**freq_steps
    wavenum = radian_freq * radian_freq / gravity
    angles = 2.0 * np.pi * np.arange(directions) / directions
    depths = -(np.arange(levels) + 0.5)
    decays = np.exp(2.0 * wavenum[:, None] * depths[None, :])
    current_weight = decays / np.sum(decays, axis=1, keepdims=True)
    drifts = (radian_freq * wavenum)[:, None] * decays
    drifts = drifts / np.sum(drifts, axis=0, keepdims=True)
    return (angles, current_weight.astype(np.float32), drifts)


def wave_kernel(
    ranks,
    cores,
    dirs,
    freqs,
    chunks,
    tile,
    u_hbm,
    v_hbm,
    weight_hbm,
    wind_hbm,
    dissipation_hbm,
    spread_hbm,
    spectrum_hbm,
    transfer_hbm,
    sea_hbm,
    courant_hbm,
    west_hbm,
    east_hbm,
    drift_hbm,
    waves_hbm,
    stokes_hbm,
    waves_ref,
    stokes_ref,
    u_ref,
    v_ref,
    weight_ref,
    wind_ref,
    dissipation_ref,
    spread_ref,
    spectrum_ref,
    transfer_ref,
    sea_ref,
    courant_ref,
    west_order,
    east_order,
    drift_ref,
    gain_ref,
    damping_ref,
    held,
    flow_send,
    flow_recv,
    flow_x,
    flow_y,
    send,
    recv,
    edge_send,
    west_first,
    east_first,
    west_second,
    east_second,
    order,
    ghosts,
    load_sem,
    waves_sem,
    stokes_sem,
    send_sem,
    recv_sem,
    flow_send_sem,
    flow_recv_sem,
    edge_send_sem,
    edge_recv_sem,
):
    edge_recv = ((west_first, east_first), (west_second, east_second))
    groups = ranks * cores
    padded = send.shape[2]
    piece = padded // chunks
    rows = recv.shape[1]
    columns = recv.shape[3]
    freq_count = cores * freqs
    plane, planes = lax.axis_index("grid"), lax.axis_size("grid")
    space = lax.axis_index("space")
    me = space * cores + lax.axis_index("spec")
    has_west, has_east = plane > 0, plane < planes - 1
    sides = ((0, has_east, has_west, plane + 1), (1, has_west, has_east, plane - 1))

    def device(level, block):
        return (level, block // cores, block % cores)

    barrier = pltpu.get_barrier_semaphore()
    for k in range(1, groups):
        partner = device(plane, lax.rem(me + k, groups))
        pl.semaphore_signal(barrier, inc=1, device_id=partner, device_id_type=mesh_ids)
    for _, exists, _, level in sides:

        @pl.when(exists)
        def _():
            for g in range(groups):
                pl.semaphore_signal(
                    barrier, inc=1, device_id=device(level, g), device_id_type=mesh_ids
                )

    loads = [
        pltpu.make_async_copy(source, target, load_sem.at[i])
        for i, (source, target) in enumerate(
            (
                (u_hbm, u_ref),
                (v_hbm, v_ref),
                (weight_hbm, weight_ref),
                (wind_hbm, wind_ref),
                (dissipation_hbm, dissipation_ref),
                (spread_hbm, spread_ref),
                (spectrum_hbm, spectrum_ref),
                (transfer_hbm, transfer_ref),
                (sea_hbm, sea_ref),
                (courant_hbm.at[me], courant_ref),
                (west_hbm, west_order),
                (east_hbm, east_order),
                (drift_hbm, drift_ref),
            )
        )
    ]
    for load in loads:
        load.start()

    def flow_copy(k):
        partner = lax.rem(me + k, groups)
        return pltpu.make_async_remote_copy(
            src_ref=flow_send.at[partner % cores],
            dst_ref=flow_recv.at[me],
            send_sem=flow_send_sem.at[k],
            recv_sem=flow_recv_sem.at[k],
            device_id=device(plane, partner),
            device_id_type=mesh_ids,
        )

    def piece_copy(phase, ch, k):
        partner = lax.rem(me + k, groups)
        part = pl.ds(pl.multiple_of(ch * piece, 8), piece)
        return pltpu.make_async_remote_copy(
            src_ref=send.at[phase, partner, part],
            dst_ref=recv.at[phase, me, part],
            send_sem=send_sem.at[phase, ch, k],
            recv_sem=recv_sem.at[phase, ch, k],
            device_id=device(plane, partner),
            device_id_type=mesh_ids,
        )

    def arrival(phase, ch, k):
        source = lax.rem(me + groups - k, groups)
        part = pl.ds(pl.multiple_of(ch * piece, 8), piece)
        return pltpu.make_async_remote_copy(
            src_ref=send.at[phase, source, part],
            dst_ref=recv.at[phase, source, part],
            send_sem=send_sem.at[phase, ch, k],
            recv_sem=recv_sem.at[phase, ch, k],
            device_id=device(plane, source),
            device_id_type=mesh_ids,
        )

    def edge_copy(stage, side, level, g, rank):
        return pltpu.make_async_remote_copy(
            src_ref=edge_send.at[stage, g],
            dst_ref=edge_recv[stage][side].at[rank],
            send_sem=edge_send_sem.at[stage, side, g],
            recv_sem=edge_recv_sem.at[stage, side, rank],
            device_id=device(level, g),
            device_id_type=mesh_ids,
        )

    def store_waves(ch, d):
        lines = min(piece // dirs, freqs) * rows
        part = pl.ds(pl.multiple_of(d * freqs * rows + ch * lines, 8), lines)
        return pltpu.make_async_copy(
            waves_ref.at[part], waves_hbm.at[part], waves_sem.at[ch, d]
        )

    def give_waves(ch):
        for d in range(dirs):
            store_waves(ch, d).start()

    for load in loads[:6]:
        load.wait()
    for at, current in ((0, u_ref), (1, v_ref)):
        flow = jnp.dot(
            weight_ref[...], current[...], precision=highest, preferred_element_type=jnp.float32
        )
        for c in range(cores):
            flow_send[c, at * freqs : (at + 1) * freqs, :] = flow[c * freqs : (c + 1) * freqs]

    for at, rate, factor in ((0, wind_ref, gain_ref), (1, dissipation_ref, damping_ref)):
        factor[...] = lax.dot_general(
            spread_ref[at],
            jnp.broadcast_to(rate[...], (columns, freq_count)),
            (((1,), (1,)), ((), ())),
            precision=highest,
            preferred_element_type=jnp.float32,
        )

    planes_beside = jnp.minimum(plane, 1) + jnp.minimum(planes - 1 - plane, 1)
    pl.semaphore_wait(barrier, groups - 1 + groups * planes_beside)

    for k in range(1, groups):
        flow_copy(k).start()
    flow_recv[me] = flow_send[lax.axis_index("spec")]

    natural = [
        (s * cores + c, d, (s * dirs + d) * freq_count + c * freqs)
        for s in range(ranks)
        for d in range(dirs)
        for c in range(cores)
    ]
    lane8 = lax.broadcasted_iota(jnp.int32, (8, columns), 1)
    row8 = lax.broadcasted_iota(jnp.int32, (8, columns), 0)
    ends = (row8 == 0) & (lane8 == columns - 1) | (row8 == 1) & (lane8 == 0)
    ends = ends.astype(jnp.float32)

    def sources(stage, spectra):
        phase = 2 * stage
        redist = jnp.dot(
            transfer_ref[...], spectra.astype(jnp.bfloat16), preferred_element_type=jnp.float32
        )
        energy = jnp.sum(spectra * spectra, axis=0, keepdims=True) * (1.0 / spectra.shape[0])
        held[...] = (
            sea_ref[pl.ds(me, 1), :].astype(jnp.float32)
            * (spectra * (1.0 + time_step * gain_ref[...]) + time_step * redist)
            / (1.0 + time_step * damping_ref[...] * energy)
        )
        for g, d, here in natural:
            send[phase, g, pl.ds(d, freqs, stride=dirs), :] = held[here : here + freqs, :]
        for k in range(1, groups):
            piece_copy(phase, 0, k).start()
        for g in range(groups):
            edge_send[stage, g, :, :padded] = lax.dot_general(
                ends,
                send[phase, g],
                (((1,), (1,)), ((), ())),
                precision=highest,
                preferred_element_type=jnp.float32,
            )
        for side, exists, _, level in sides:

            @pl.when(exists)
            def _():
                for g in range(groups):
                    edge_copy(stage, side, level, g, me).start()

        for ch in range(1, chunks):
            for k in range(1, groups):
                piece_copy(phase, ch, k).start()
        recv[phase, me] = send[phase, me]

    def border(stage):
        for side, _, exists, level in sides:
            wanted = (west_order, east_order)[side]

            @pl.when(exists)
            def _():
                for r in range(groups):
                    edge_copy(stage, side, level, r, r).wait_recv()
                order[...] = jnp.zeros_like(order)
                for y in range(rows):
                    order[y : y + 1, :] = edge_recv[stage][side][wanted[0, y], side : side + 1, :]
                square = (padded, padded)
                unit = lax.broadcasted_iota(jnp.int32, square, 0) == lax.broadcasted_iota(
                    jnp.int32, square, 1
                )
                ghosts[side] = lax.dot_general(
                    unit.astype(jnp.float32),
                    order[:, :padded],
                    (((1,), (1,)), ((), ())),
                    precision=highest,
                    preferred_element_type=jnp.float32,
                )

            @pl.when(jnp.logical_not(exists))
            def _():
                ghosts[side] = jnp.zeros(ghosts.shape[1:], jnp.float32)

    shape = (tile, columns)
    lane = lax.broadcasted_iota(jnp.int32, shape, 1)
    first, last = lane == 0, lane == columns - 1
    quadrant = (space * dirs) // (ranks * dirs // 4)
    onward = (quadrant == 0) | (quadrant == 3)
    ahead = onward.astype(jnp.int32)
    place = ahead * lane + (1 - ahead) * (columns - 1 - lane)

    def rolled(block, turn):
        flat = pltpu.roll(block.reshape(-1, columns), turn, 1)
        return flat.reshape(block.shape)

    def sweep(phase, base):
        part = pl.ds(pl.multiple_of(base, 8), tile)
        wave = recv[phase, :, part, :]
        a, b = flow_x[:, part, :], flow_y[:, part, :]
        cx = jnp.broadcast_to(courant_ref[0, part, :], shape)
        cy = jnp.broadcast_to(courant_ref[1, part, :], shape)
        raw_west, raw_east = ghosts[0, part, :], ghosts[1, part, :]
        ghost_west = jnp.stack(
            [
                jnp.where(first, pltpu.roll(raw_west, (columns - y) % columns, 1), 0.0)
                for y in range(rows)
            ]
        )
        ghost_east = jnp.stack(
            [
                jnp.where(last, pltpu.roll(raw_east, columns - 1 - y, 1), 0.0)
                for y in range(rows)
            ]
        )
        blank = jnp.zeros((1,) + shape, jnp.float32)
        west = jnp.where(first[None], ghost_west, rolled(wave, 1))
        east = jnp.where(last[None], ghost_east, rolled(wave, columns - 1))
        north = jnp.concatenate([blank, wave[:-1]], axis=0)
        south = jnp.concatenate([wave[1:], blank], axis=0)
        moved = (
            wave
            - jnp.maximum(a, 0.0) * (wave - west)
            - jnp.maximum(-a, 0.0) * (wave - east)
            - jnp.maximum(b, 0.0) * (wave - north)
            - jnp.maximum(-b, 0.0) * (wave - south)
            + jnp.maximum(cx, 0.0)[None] * ghost_west
            + jnp.maximum(-cx, 0.0)[None] * ghost_east
        )
        speed = jnp.abs(cx)
        scale = 1.0 / (1.0 + speed)
        ratio = speed * scale
        swept = moved * scale[None]
        step = 1
        while step < columns:
            turn = ahead * step + (1 - ahead) * (columns - step)
            swept = swept + jnp.where(place >= step, ratio, 0.0)[None] * rolled(swept, turn)
            ratio = ratio * ratio
            step *= 2
        scale = 1.0 / (1.0 + jnp.abs(cy))
        down, up = jnp.maximum(cy, 0.0) * scale, jnp.maximum(-cy, 0.0) * scale
        lines = [swept[y] * scale for y in range(rows)]
        for y in range(1, rows):
            lines[y] = lines[y] + down * lines[y - 1]
        for y in range(rows - 2, -1, -1):
            lines[y] = lines[y] + up * lines[y + 1]
        return [sea_ref[y : y + 1, :].astype(jnp.float32) * lines[y] for y in range(rows)]

    def propagate(phase, emit, after):
        def chunk(ch, carry):
            for k in range(1, groups):
                arrival(phase, ch, k).wait_recv()
            for t in range(piece // tile):
                base = ch * piece + t * tile
                emit(base, sweep(phase, base))
            after(ch)
            return carry

        lax.fori_loop(0, chunks, chunk, 0)

    def emit_send(base, lines):
        for y in range(rows):
            send[1, y, pl.ds(pl.multiple_of(base, 8), tile), :] = lines[y]

    def send_piece(ch):
        for k in range(1, groups):
            piece_copy(1, ch, k).start()
        part = pl.ds(pl.multiple_of(ch * piece, 8), piece)
        recv[1, me, part, :] = send[1, me, part, :]

    def emit_waves(base, lines):
        freq = base // dirs
        for y in range(rows):
            for f in range(min(tile // dirs, freqs)):
                waves_ref[pl.ds((freq + f) * rows + y, dirs, stride=freqs * rows), :] = lines[y][
                    f * dirs : (f + 1) * dirs
                ]

    for load in loads[6:-1]:
        load.wait()
    sources(0, spectrum_ref[...])
    for k in range(1, groups):
        source = lax.rem(me + groups - k, groups)
        pltpu.make_async_remote_copy(
            src_ref=flow_send.at[0],
            dst_ref=flow_recv.at[source],
            send_sem=flow_send_sem.at[k],
            recv_sem=flow_recv_sem.at[k],
            device_id=device(plane, source),
            device_id_type=mesh_ids,
        ).wait_recv()
    for f in range(freqs):
        wide = (rows, dirs, columns)
        flow_x[:, f * dirs : (f + 1) * dirs, :] = jnp.broadcast_to(
            flow_recv[:, f : f + 1, :], wide
        )
        flow_y[:, f * dirs : (f + 1) * dirs, :] = jnp.broadcast_to(
            flow_recv[:, freqs + f : freqs + f + 1, :], wide
        )
    border(0)
    propagate(0, emit_send, send_piece)
    for k in range(1, groups):
        for ch in range(chunks):
            arrival(1, ch, k).wait_recv()
    for g, d, here in natural:
        held[here : here + freqs, :] = recv[1, g, pl.ds(d, freqs, stride=dirs), :]
    sources(1, held[...])
    loads[-1].wait()
    stokes_ref[...] = jnp.dot(
        drift_ref[...], held[...], precision=highest, preferred_element_type=jnp.float32
    )
    stokes_store = pltpu.make_async_copy(stokes_ref, stokes_hbm, stokes_sem)
    stokes_store.start()
    border(1)
    propagate(2, emit_waves, give_waves)

    for ch in range(chunks):
        for d in range(dirs):
            store_waves(ch, d).wait()
    stokes_store.wait()
    for k in range(1, groups):
        flow_copy(k).wait_send()
        for phase in range(3):
            for ch in range(chunks):
                piece_copy(phase, ch, k).wait_send()
    for stage in range(2):
        for side, exists, _, level in sides:

            @pl.when(exists)
            def _():
                for g in range(groups):
                    edge_copy(stage, side, level, g, me).wait_send()


def rounded_up(count, unit):
    return -(-count // unit) * unit


def shards(
    spectrum,
    land_sea,
    west_index,
    east_index,
    current_u,
    current_v,
    transfer,
    wind_rate,
    dissipation,
):
    ranks = lax.axis_size("space")
    cores = lax.axis_size("spec")
    directions, freq_count, rows_local, columns = spectrum.shape[1:]
    levels = current_u.shape[1]
    total_rows = land_sea.shape[1]
    dir_local = directions // ranks
    freq_local = freq_count // cores
    components = directions * freq_count
    comps_local = dir_local * freq_local
    groups = ranks * cores
    padded = rounded_up(comps_local, 8)
    tile = 24 if padded % 24 == 0 else 8
    chunks = 3 if padded % (3 * tile) == 0 else 1
    width = rounded_up(padded, 128)
    flow_rows = rounded_up(2 * freq_local, 8)
    angles, current_weight, drifts = tables(freq_count, directions, levels)
    cosines, sines = np.cos(angles), np.sin(angles)
    cosines[np.abs(cosines) < 1e-12] = 0.0
    sines[np.abs(sines) < 1e-12] = 0.0
    speeds = courant_scale * growth ** (-np.arange(freq_count).astype(np.float64))
    courant = np.stack([cosines[:, None] * speeds[None, :], sines[:, None] * speeds[None, :]])
    courant = courant.reshape(2, ranks, dir_local, cores, freq_local).transpose(1, 3, 0, 4, 2)
    courant = courant.reshape(groups, 2, comps_local, 1).astype(np.float32)
    courant = np.pad(courant, ((0, 0), (0, 0), (0, padded - comps_local), (0, 0)))

    trig = np.stack([cosines, sines]) * stokes_gain / math.sqrt(directions)
    stokes_table = trig[:, None, :, None] * drifts.T[None, :, None, :]
    stokes_table = stokes_table.reshape(2 * levels, components).astype(np.float32)

    heading = np.repeat(0.5 * (1.0 + cosines), freq_count)[:, None]
    unit = np.tile(np.eye(freq_count), (directions, 1))
    spread = np.stack([heading * unit, unit]).astype(np.float32)
    f32 = jnp.float32
    waves, stokes = pl.pallas_call(
        functools.partial(
            wave_kernel, ranks, cores, dir_local, freq_local, chunks, tile
        ),
        out_shape=(
            jax.ShapeDtypeStruct((comps_local * total_rows, columns), f32),
            jax.ShapeDtypeStruct((2 * levels, columns), f32),
        ),
        in_specs=[in_place] * 13,
        out_specs=(in_place, in_place),
        scratch_shapes=[
            pltpu.VMEM((comps_local * total_rows, columns), f32),
            pltpu.VMEM((2 * levels, columns), f32),
            pltpu.VMEM((levels, columns), f32),
            pltpu.VMEM((levels, columns), f32),
            pltpu.VMEM(current_weight.shape, f32),
            pltpu.VMEM((1, freq_count), f32),
            pltpu.VMEM((1, freq_count), f32),
            pltpu.VMEM(spread.shape, f32),
            pltpu.VMEM((components, columns), f32),
            pltpu.VMEM(transfer.shape, transfer.dtype),
            pltpu.VMEM(land_sea.shape[1:], land_sea.dtype),
            pltpu.VMEM(courant.shape[1:], f32),
            pltpu.SMEM(west_index.shape, west_index.dtype),
            pltpu.SMEM(east_index.shape, east_index.dtype),
            pltpu.VMEM(stokes_table.shape, f32),
            pltpu.VMEM((components, columns), f32),
            pltpu.VMEM((components, columns), f32),
            pltpu.VMEM((components, columns), f32),
            pltpu.VMEM((cores, flow_rows, columns), f32),
            pltpu.VMEM((groups, flow_rows, columns), f32),
            pltpu.VMEM((groups, padded, columns), f32),
            pltpu.VMEM((groups, padded, columns), f32),
            pltpu.VMEM((3, groups, padded, columns), f32),
            pltpu.VMEM((3, groups, padded, columns), f32),
            pltpu.VMEM((2, groups, 8, width), f32),
            pltpu.VMEM((groups, 8, width), f32),
            pltpu.VMEM((groups, 8, width), f32),
            pltpu.VMEM((groups, 8, width), f32),
            pltpu.VMEM((groups, 8, width), f32),
            pltpu.VMEM((columns, width), f32),
            pltpu.VMEM((2, padded, columns), f32),
            pltpu.SemaphoreType.DMA((13,)),
            pltpu.SemaphoreType.DMA((chunks, dir_local)),
            pltpu.SemaphoreType.DMA(()),
            pltpu.SemaphoreType.DMA((3, chunks, groups)),
            pltpu.SemaphoreType.DMA((3, chunks, groups)),
            pltpu.SemaphoreType.DMA((groups,)),
            pltpu.SemaphoreType.DMA((groups,)),
            pltpu.SemaphoreType.DMA((2, 2, groups)),
            pltpu.SemaphoreType.DMA((2, 2, groups)),
        ],
        compiler_params=pltpu.CompilerParams(
            collective_id=0, has_side_effects=True, vmem_limit_bytes=64 * 1024 * 1024
        ),
        name="waves",
    )(
        current_u[0].reshape(levels, columns),
        current_v[0].reshape(levels, columns),
        jnp.asarray(current_weight),
        wind_rate.reshape(1, freq_count),
        dissipation.reshape(1, freq_count),
        jnp.asarray(spread),
        spectrum[0].reshape(components, columns),
        transfer,
        land_sea[0],
        jnp.asarray(courant),
        west_index,
        east_index,
        jnp.asarray(stokes_table),
    )
    return (
        waves.reshape(1, dir_local, freq_local, total_rows, columns),
        stokes.reshape(1, 2 * levels, rows_local, columns),
    )


def solution(mesh):
    placed = (
        P("grid", None, None, ("space", "spec"), None),
        P("grid", None, None),
        P("grid", None),
        P("grid", None),
        P("grid", None, ("space", "spec"), None),
        P("grid", None, ("space", "spec"), None),
        P(),
        P(),
        P(),
    )
    return jax.shard_map(
        shards,
        mesh=mesh,
        in_specs=placed,
        out_specs=(
            P("grid", "space", "spec", None, None),
            P("grid", None, ("space", "spec"), None),
        ),
        check_vma=False,
    )
```

```python
import functools
import math

import jax
import jax.numpy as jnp
import numpy as np
from jax import lax
from jax.experimental import pallas as pl
from jax.experimental.pallas import tpu as pltpu
from jax.sharding import PartitionSpec as P

sigma_base = 0.2199
gravity = 9.81
growth = 1.1
courant_scale = 3.0
time_step = 0.5
stokes_gain = 2.0
highest = lax.Precision.HIGHEST
mesh_ids = pl.DeviceIdType.MESH
in_place = pl.BlockSpec(memory_space=pltpu.HBM)


def tables(freq_count, directions, levels):
    freq_steps = np.arange(freq_count).astype(np.float64)
    radian_freq = sigma_base * growth**freq_steps
    wavenum = radian_freq * radian_freq / gravity
    angles = 2.0 * np.pi * np.arange(directions) / directions
    depths = -(np.arange(levels) + 0.5)
    decays = np.exp(2.0 * wavenum[:, None] * depths[None, :])
    current_weight = decays / np.sum(decays, axis=1, keepdims=True)
    drifts = (radian_freq * wavenum)[:, None] * decays
    drifts = drifts / np.sum(drifts, axis=0, keepdims=True)
    return (angles, current_weight.astype(np.float32), drifts)


def wave_kernel(
    ranks,
    cores,
    dirs,
    freqs,
    chunks,
    tile,
    u_hbm,
    v_hbm,
    weight_hbm,
    wind_hbm,
    dissipation_hbm,
    spread_hbm,
    spectrum_hbm,
    transfer_hbm,
    sea_hbm,
    courant_hbm,
    west_hbm,
    east_hbm,
    drift_hbm,
    waves_hbm,
    stokes_hbm,
    waves_ref,
    stokes_ref,
    u_ref,
    v_ref,
    weight_ref,
    wind_ref,
    dissipation_ref,
    spread_ref,
    spectrum_ref,
    transfer_ref,
    sea_ref,
    courant_ref,
    west_order,
    east_order,
    drift_ref,
    gain_ref,
    damping_ref,
    held,
    flow_send,
    flow_recv,
    flow_x,
    flow_y,
    send,
    recv,
    edge_send,
    west_first,
    east_first,
    west_second,
    east_second,
    order,
    ghosts,
    load_sem,
    waves_sem,
    stokes_sem,
    send_sem,
    recv_sem,
    flow_send_sem,
    flow_recv_sem,
    edge_send_sem,
    edge_recv_sem,
):
    edge_recv = ((west_first, east_first), (west_second, east_second))
    groups = ranks * cores
    padded = send.shape[2]
    piece = padded // chunks
    rows = recv.shape[1]
    columns = recv.shape[3]
    freq_count = cores * freqs
    plane, planes = lax.axis_index("grid"), lax.axis_size("grid")
    space = lax.axis_index("space")
    me = space * cores + lax.axis_index("spec")
    has_west, has_east = plane > 0, plane < planes - 1
    sides = ((0, has_east, has_west, plane + 1), (1, has_west, has_east, plane - 1))

    def device(level, block):
        return (level, block // cores, block % cores)

    barrier = pltpu.get_barrier_semaphore()
    for k in range(1, groups):
        partner = device(plane, lax.rem(me + k, groups))
        pl.semaphore_signal(barrier, inc=1, device_id=partner, device_id_type=mesh_ids)
    for _, exists, _, level in sides:

        @pl.when(exists)
        def _():
            for g in range(groups):
                pl.semaphore_signal(
                    barrier, inc=1, device_id=device(level, g), device_id_type=mesh_ids
                )

    loads = [
        pltpu.make_async_copy(source, target, load_sem.at[i])
        for i, (source, target) in enumerate(
            (
                (u_hbm, u_ref),
                (v_hbm, v_ref),
                (weight_hbm, weight_ref),
                (wind_hbm, wind_ref),
                (dissipation_hbm, dissipation_ref),
                (spread_hbm, spread_ref),
                (spectrum_hbm, spectrum_ref),
                (transfer_hbm, transfer_ref),
                (sea_hbm, sea_ref),
                (courant_hbm.at[me], courant_ref),
                (west_hbm, west_order),
                (east_hbm, east_order),
                (drift_hbm, drift_ref),
            )
        )
    ]
    for load in loads:
        load.start()

    def flow_copy(k):
        partner = lax.rem(me + k, groups)
        return pltpu.make_async_remote_copy(
            src_ref=flow_send.at[partner % cores],
            dst_ref=flow_recv.at[me],
            send_sem=flow_send_sem.at[k],
            recv_sem=flow_recv_sem.at[k],
            device_id=device(plane, partner),
            device_id_type=mesh_ids,
        )

    def piece_copy(phase, ch, k):
        partner = lax.rem(me + k, groups)
        part = pl.ds(pl.multiple_of(ch * piece, 8), piece)
        return pltpu.make_async_remote_copy(
            src_ref=send.at[phase, partner, part],
            dst_ref=recv.at[phase, me, part],
            send_sem=send_sem.at[phase, ch, k],
            recv_sem=recv_sem.at[phase, ch, k],
            device_id=device(plane, partner),
            device_id_type=mesh_ids,
        )

    def arrival(phase, ch, k):
        source = lax.rem(me + groups - k, groups)
        part = pl.ds(pl.multiple_of(ch * piece, 8), piece)
        return pltpu.make_async_remote_copy(
            src_ref=send.at[phase, source, part],
            dst_ref=recv.at[phase, source, part],
            send_sem=send_sem.at[phase, ch, k],
            recv_sem=recv_sem.at[phase, ch, k],
            device_id=device(plane, source),
            device_id_type=mesh_ids,
        )

    def edge_copy(stage, side, level, g, rank):
        return pltpu.make_async_remote_copy(
            src_ref=edge_send.at[stage, g],
            dst_ref=edge_recv[stage][side].at[rank],
            send_sem=edge_send_sem.at[stage, side, g],
            recv_sem=edge_recv_sem.at[stage, side, rank],
            device_id=device(level, g),
            device_id_type=mesh_ids,
        )

    def store_waves(ch, d):
        lines = min(piece // dirs, freqs) * rows
        part = pl.ds(pl.multiple_of(d * freqs * rows + ch * lines, 8), lines)
        return pltpu.make_async_copy(
            waves_ref.at[part], waves_hbm.at[part], waves_sem.at[ch, d]
        )

    def give_waves(ch):
        for d in range(dirs):
            store_waves(ch, d).start()

    for load in loads[:6]:
        load.wait()
    for at, current in ((0, u_ref), (1, v_ref)):
        flow = jnp.dot(
            weight_ref[...], current[...], precision=highest, preferred_element_type=jnp.float32
        )
        for c in range(cores):
            flow_send[c, at * freqs : (at + 1) * freqs, :] = flow[c * freqs : (c + 1) * freqs]

    for at, rate, factor in ((0, wind_ref, gain_ref), (1, dissipation_ref, damping_ref)):
        factor[...] = lax.dot_general(
            spread_ref[at],
            jnp.broadcast_to(rate[...], (columns, freq_count)),
            (((1,), (1,)), ((), ())),
            precision=highest,
            preferred_element_type=jnp.float32,
        )

    planes_beside = jnp.minimum(plane, 1) + jnp.minimum(planes - 1 - plane, 1)
    pl.semaphore_wait(barrier, groups - 1 + groups * planes_beside)

    for k in range(1, groups):
        flow_copy(k).start()
    flow_recv[me] = flow_send[lax.axis_index("spec")]

    natural = [
        (s * cores + c, d, (s * dirs + d) * freq_count + c * freqs)
        for s in range(ranks)
        for d in range(dirs)
        for c in range(cores)
    ]
    lane8 = lax.broadcasted_iota(jnp.int32, (8, columns), 1)
    row8 = lax.broadcasted_iota(jnp.int32, (8, columns), 0)
    ends = (row8 == 0) & (lane8 == columns - 1) | (row8 == 1) & (lane8 == 0)
    ends = ends.astype(jnp.float32)

    def sources(stage, spectra):
        phase = 2 * stage
        redist = jnp.dot(
            transfer_ref[...], spectra.astype(jnp.bfloat16), preferred_element_type=jnp.float32
        )
        energy = jnp.sum(spectra * spectra, axis=0, keepdims=True) * (1.0 / spectra.shape[0])
        held[...] = (
            sea_ref[pl.ds(me, 1), :].astype(jnp.float32)
            * (spectra * (1.0 + time_step * gain_ref[...]) + time_step * redist)
            / (1.0 + time_step * damping_ref[...] * energy)
        )
        for g, d, here in natural:
            send[phase, g, pl.ds(d, freqs, stride=dirs), :] = held[here : here + freqs, :]
        for k in range(1, groups):
            piece_copy(phase, 0, k).start()
        for g in range(groups):
            edge_send[stage, g, :, :padded] = lax.dot_general(
                ends,
                send[phase, g],
                (((1,), (1,)), ((), ())),
                precision=highest,
                preferred_element_type=jnp.float32,
            )
        for side, exists, _, level in sides:

            @pl.when(exists)
            def _():
                for g in range(groups):
                    edge_copy(stage, side, level, g, me).start()

        for ch in range(1, chunks):
            for k in range(1, groups):
                piece_copy(phase, ch, k).start()
        recv[phase, me] = send[phase, me]

    def border(stage):
        for side, _, exists, level in sides:
            wanted = (west_order, east_order)[side]

            @pl.when(exists)
            def _():
                for r in range(groups):
                    edge_copy(stage, side, level, r, r).wait_recv()
                order[...] = jnp.zeros_like(order)
                for y in range(rows):
                    order[y : y + 1, :] = edge_recv[stage][side][wanted[0, y], side : side + 1, :]
                square = (padded, padded)
                unit = lax.broadcasted_iota(jnp.int32, square, 0) == lax.broadcasted_iota(
                    jnp.int32, square, 1
                )
                ghosts[side] = lax.dot_general(
                    unit.astype(jnp.float32),
                    order[:, :padded],
                    (((1,), (1,)), ((), ())),
                    precision=highest,
                    preferred_element_type=jnp.float32,
                )

            @pl.when(jnp.logical_not(exists))
            def _():
                ghosts[side] = jnp.zeros(ghosts.shape[1:], jnp.float32)

    shape = (tile, columns)
    lane = lax.broadcasted_iota(jnp.int32, shape, 1)
    first, last = lane == 0, lane == columns - 1
    quadrant = (space * dirs) // (ranks * dirs // 4)
    onward = (quadrant == 0) | (quadrant == 3)
    ahead = onward.astype(jnp.int32)
    place = ahead * lane + (1 - ahead) * (columns - 1 - lane)

    def rolled(block, turn):
        flat = pltpu.roll(block.reshape(-1, columns), turn, 1)
        return flat.reshape(block.shape)

    def sweep(phase, base):
        part = pl.ds(pl.multiple_of(base, 8), tile)
        wave = recv[phase, :, part, :]
        a, b = flow_x[:, part, :], flow_y[:, part, :]
        cx = jnp.broadcast_to(courant_ref[0, part, :], shape)
        cy = jnp.broadcast_to(courant_ref[1, part, :], shape)
        raw_west, raw_east = ghosts[0, part, :], ghosts[1, part, :]
        ghost_west = jnp.stack(
            [
                jnp.where(first, pltpu.roll(raw_west, (columns - y) % columns, 1), 0.0)
                for y in range(rows)
            ]
        )
        ghost_east = jnp.stack(
            [
                jnp.where(last, pltpu.roll(raw_east, columns - 1 - y, 1), 0.0)
                for y in range(rows)
            ]
        )
        blank = jnp.zeros((1,) + shape, jnp.float32)
        west = jnp.where(first[None], ghost_west, rolled(wave, 1))
        east = jnp.where(last[None], ghost_east, rolled(wave, columns - 1))
        north = jnp.concatenate([blank, wave[:-1]], axis=0)
        south = jnp.concatenate([wave[1:], blank], axis=0)
        moved = (
            wave
            - jnp.maximum(a, 0.0) * (wave - west)
            - jnp.maximum(-a, 0.0) * (wave - east)
            - jnp.maximum(b, 0.0) * (wave - north)
            - jnp.maximum(-b, 0.0) * (wave - south)
            + jnp.maximum(cx, 0.0)[None] * ghost_west
            + jnp.maximum(-cx, 0.0)[None] * ghost_east
        )
        speed = jnp.abs(cx)
        scale = 1.0 / (1.0 + speed)
        ratio = speed * scale
        swept = moved * scale[None]
        step = 1
        while step < columns:
            turn = ahead * step + (1 - ahead) * (columns - step)
            swept = swept + jnp.where(place >= step, ratio, 0.0)[None] * rolled(swept, turn)
            ratio = ratio * ratio
            step *= 2
        scale = 1.0 / (1.0 + jnp.abs(cy))
        down, up = jnp.maximum(cy, 0.0) * scale, jnp.maximum(-cy, 0.0) * scale
        lines = [swept[y] * scale for y in range(rows)]
        for y in range(1, rows):
            lines[y] = lines[y] + down * lines[y - 1]
        for y in range(rows - 2, -1, -1):
            lines[y] = lines[y] + up * lines[y + 1]
        return lines

    def propagate(phase, emit, after):
        def chunk(ch, carry):
            for k in range(1, groups):
                arrival(phase, ch, k).wait_recv()
            for t in range(piece // tile):
                base = ch * piece + t * tile
                emit(base, sweep(phase, base))
            after(ch)
            return carry

        lax.fori_loop(0, chunks, chunk, 0)

    def emit_send(base, lines):
        for y in range(rows):
            sea = sea_ref[y : y + 1, :].astype(jnp.float32)
            send[1, y, pl.ds(pl.multiple_of(base, 8), tile), :] = sea * lines[y]

    def send_piece(ch):
        for k in range(1, groups):
            piece_copy(1, ch, k).start()
        part = pl.ds(pl.multiple_of(ch * piece, 8), piece)
        recv[1, me, part, :] = send[1, me, part, :]

    def emit_waves(base, lines):
        freq = base // dirs
        for y in range(rows):
            for f in range(min(tile // dirs, freqs)):
                waves_ref[pl.ds((freq + f) * rows + y, dirs, stride=freqs * rows), :] = lines[y][
                    f * dirs : (f + 1) * dirs
                ]

    for load in loads[6:-1]:
        load.wait()
    sources(0, spectrum_ref[...])
    for k in range(1, groups):
        source = lax.rem(me + groups - k, groups)
        pltpu.make_async_remote_copy(
            src_ref=flow_send.at[0],
            dst_ref=flow_recv.at[source],
            send_sem=flow_send_sem.at[k],
            recv_sem=flow_recv_sem.at[k],
            device_id=device(plane, source),
            device_id_type=mesh_ids,
        ).wait_recv()
    for f in range(freqs):
        wide = (rows, dirs, columns)
        flow_x[:, f * dirs : (f + 1) * dirs, :] = jnp.broadcast_to(
            flow_recv[:, f : f + 1, :], wide
        )
        flow_y[:, f * dirs : (f + 1) * dirs, :] = jnp.broadcast_to(
            flow_recv[:, freqs + f : freqs + f + 1, :], wide
        )
    border(0)
    propagate(0, emit_send, send_piece)
    for k in range(1, groups):
        for ch in range(chunks):
            arrival(1, ch, k).wait_recv()
    for g, d, here in natural:
        held[here : here + freqs, :] = recv[1, g, pl.ds(d, freqs, stride=dirs), :]
    sources(1, held[...])
    loads[-1].wait()
    stokes_ref[...] = jnp.dot(
        drift_ref[...], held[...], precision=highest, preferred_element_type=jnp.float32
    )
    stokes_store = pltpu.make_async_copy(stokes_ref, stokes_hbm, stokes_sem)
    stokes_store.start()
    border(1)
    propagate(2, emit_waves, give_waves)

    for ch in range(chunks):
        for d in range(dirs):
            store_waves(ch, d).wait()
    stokes_store.wait()
    for k in range(1, groups):
        flow_copy(k).wait_send()
        for phase in range(3):
            for ch in range(chunks):
                piece_copy(phase, ch, k).wait_send()
    for stage in range(2):
        for side, exists, _, level in sides:

            @pl.when(exists)
            def _():
                for g in range(groups):
                    edge_copy(stage, side, level, g, me).wait_send()


def rounded_up(count, unit):
    return -(-count // unit) * unit


def shards(
    spectrum,
    land_sea,
    west_index,
    east_index,
    current_u,
    current_v,
    transfer,
    wind_rate,
    dissipation,
):
    ranks = lax.axis_size("space")
    cores = lax.axis_size("spec")
    directions, freq_count, rows_local, columns = spectrum.shape[1:]
    levels = current_u.shape[1]
    total_rows = land_sea.shape[1]
    dir_local = directions // ranks
    freq_local = freq_count // cores
    components = directions * freq_count
    comps_local = dir_local * freq_local
    groups = ranks * cores
    padded = rounded_up(comps_local, 8)
    tile = 24 if padded % 24 == 0 else 8
    chunks = 6 if padded % (6 * tile) == 0 else 1
    width = rounded_up(padded, 128)
    flow_rows = rounded_up(2 * freq_local, 8)
    angles, current_weight, drifts = tables(freq_count, directions, levels)
    cosines, sines = np.cos(angles), np.sin(angles)
    cosines[np.abs(cosines) < 1e-12] = 0.0
    sines[np.abs(sines) < 1e-12] = 0.0
    speeds = courant_scale * growth ** (-np.arange(freq_count).astype(np.float64))
    courant = np.stack([cosines[:, None] * speeds[None, :], sines[:, None] * speeds[None, :]])
    courant = courant.reshape(2, ranks, dir_local, cores, freq_local).transpose(1, 3, 0, 4, 2)
    courant = courant.reshape(groups, 2, comps_local, 1).astype(np.float32)
    courant = np.pad(courant, ((0, 0), (0, 0), (0, padded - comps_local), (0, 0)))

    trig = np.stack([cosines, sines])
    stokes_table = trig[:, None, :, None] * drifts.T[None, :, None, :]
    stokes_table = stokes_table.reshape(2 * levels, components).astype(np.float32)

    heading = np.repeat(0.5 * (1.0 + cosines), freq_count)[:, None]
    unit = np.tile(np.eye(freq_count), (directions, 1))
    spread = np.stack([heading * unit, unit]).astype(np.float32)
    f32 = jnp.float32
    waves, stokes = pl.pallas_call(
        functools.partial(
            wave_kernel, ranks, cores, dir_local, freq_local, chunks, tile
        ),
        out_shape=(
            jax.ShapeDtypeStruct((comps_local * total_rows, columns), f32),
            jax.ShapeDtypeStruct((2 * levels, columns), f32),
        ),
        in_specs=[in_place] * 13,
        out_specs=(in_place, in_place),
        scratch_shapes=[
            pltpu.VMEM((comps_local * total_rows, columns), f32),
            pltpu.VMEM((2 * levels, columns), f32),
            pltpu.VMEM((levels, columns), f32),
            pltpu.VMEM((levels, columns), f32),
            pltpu.VMEM(current_weight.shape, f32),
            pltpu.VMEM((1, freq_count), f32),
            pltpu.VMEM((1, freq_count), f32),
            pltpu.VMEM(spread.shape, f32),
            pltpu.VMEM((components, columns), f32),
            pltpu.VMEM(transfer.shape, transfer.dtype),
            pltpu.VMEM(land_sea.shape[1:], land_sea.dtype),
            pltpu.VMEM(courant.shape[1:], f32),
            pltpu.SMEM(west_index.shape, west_index.dtype),
            pltpu.SMEM(east_index.shape, east_index.dtype),
            pltpu.VMEM(stokes_table.shape, f32),
            pltpu.VMEM((components, columns), f32),
            pltpu.VMEM((components, columns), f32),
            pltpu.VMEM((components, columns), f32),
            pltpu.VMEM((cores, flow_rows, columns), f32),
            pltpu.VMEM((groups, flow_rows, columns), f32),
            pltpu.VMEM((groups, padded, columns), f32),
            pltpu.VMEM((groups, padded, columns), f32),
            pltpu.VMEM((3, groups, padded, columns), f32),
            pltpu.VMEM((3, groups, padded, columns), f32),
            pltpu.VMEM((2, groups, 8, width), f32),
            pltpu.VMEM((groups, 8, width), f32),
            pltpu.VMEM((groups, 8, width), f32),
            pltpu.VMEM((groups, 8, width), f32),
            pltpu.VMEM((groups, 8, width), f32),
            pltpu.VMEM((columns, width), f32),
            pltpu.VMEM((2, padded, columns), f32),
            pltpu.SemaphoreType.DMA((13,)),
            pltpu.SemaphoreType.DMA((chunks, dir_local)),
            pltpu.SemaphoreType.DMA(()),
            pltpu.SemaphoreType.DMA((3, chunks, groups)),
            pltpu.SemaphoreType.DMA((3, chunks, groups)),
            pltpu.SemaphoreType.DMA((groups,)),
            pltpu.SemaphoreType.DMA((groups,)),
            pltpu.SemaphoreType.DMA((2, 2, groups)),
            pltpu.SemaphoreType.DMA((2, 2, groups)),
        ],
        compiler_params=pltpu.CompilerParams(
            collective_id=0, has_side_effects=True, vmem_limit_bytes=64 * 1024 * 1024
        ),
        name="waves",
    )(
        current_u[0].reshape(levels, columns),
        current_v[0].reshape(levels, columns),
        jnp.asarray(current_weight),
        wind_rate.reshape(1, freq_count),
        dissipation.reshape(1, freq_count),
        jnp.asarray(spread),
        spectrum[0].reshape(components, columns),
        transfer,
        land_sea[0],
        jnp.asarray(courant),
        west_index,
        east_index,
        jnp.asarray(stokes_table),
    )
    waves = waves.reshape(1, dir_local, freq_local, total_rows, columns)
    stokes = stokes.reshape(1, 2 * levels, rows_local, columns)
    return (
        waves * land_sea[0].astype(f32),
        stokes * np.float32(stokes_gain / math.sqrt(directions)),
    )


def solution(mesh):
    placed = (
        P("grid", None, None, ("space", "spec"), None),
        P("grid", None, None),
        P("grid", None),
        P("grid", None),
        P("grid", None, ("space", "spec"), None),
        P("grid", None, ("space", "spec"), None),
        P(),
        P(),
        P(),
    )
    return jax.shard_map(
        shards,
        mesh=mesh,
        in_specs=placed,
        out_specs=(
            P("grid", "space", "spec", None, None),
            P("grid", None, ("space", "spec"), None),
        ),
        check_vma=False,
    )
```
